256 devices in a mesh: row: 8 (over y, z_lo), tm: 32 (over x, z_hi, core).
Axes of the slice: x: 4, y: 4, z: 8 (z_hi: 4, z_lo: 2; z = z_hi * 2 + z_lo), core: 2. Of those that a mesh axis runs over, the one named last changes fastest.
Arguments:
- occ_factor: float32 [32, 2048, 2048], P('tm', 'row'), may hold values from -0.077339804 to 0.077339804
- vir_factor: float32 [32, 2048, 2048], P('tm', 'row'), may hold values from -0.077339804 to 0.077339804
- eps_basis: float32 [2048, 1024], P('row'), may hold values from -0.125 to 0.125
Outputs:
- screened: float32 [32, 1024, 1024], P('tm', 'row')
The draws below stay inside these ranges and needn't reach their ends.
All inputs are finite; a program needn't handle non-finite values.
Results may differ from the reference program's by a relative error of at most 0.000075.
Values sent between devices are 32-bit elements; how exact they have to be, the bound alone decides.
A program may use at most 128 MiB of HBM per device.

```python
import jax
import jax.numpy as jnp
from jax import lax

NOCC = 2048
NVIR = 2048
NEPS = 1024
NT = 32
NAUX = 2048


def factor_draw(key, width, salt):
    common = jax.random.normal(jax.random.fold_in(key, salt + 1), (NT, 1, width), jnp.float32)
    private = jax.random.normal(jax.random.fold_in(key, salt + 2), (NT, NAUX, width), jnp.float32)
    values = jnp.clip((common + private) * 0.7071, -3.5, 3.5)
    return (values / jnp.sqrt(jnp.float32(width))).astype(jnp.float32)


def draw_occ_factor(key, part):
    return factor_draw(key, NOCC, 110)


def draw_vir_factor(key, part):
    return factor_draw(key, NVIR, 220)


def steps_of(own_key, extent, split, low, high):
    def one(dim, shards_of):
        steps = jax.random.uniform(jax.random.fold_in(jax.random.fold_in(own_key, 6), dim), (shards_of,), jnp.float32, low / len(split), high / len(split))
        return jnp.repeat(jnp.exp(steps), extent[dim] // shards_of).reshape((-1,) + (1,) * (len(extent) - dim - 1))

    loudness = one(*split[0])
    for cut in split[1:]:
        loudness = loudness * one(*cut)
    return loudness


def centred(rng, shape, deviation, reach, shards=(), held_as=jnp.bfloat16):
    result = deviation * jax.random.normal(rng, shape, jnp.float32)
    if shards:
        result = result * steps_of(rng, shape, shards, -0.22, 0.18)
    return jnp.clip(result, -reach, reach).astype(held_as)


def setup_inputs(seed: int = 0) -> dict:
    seeds = jax.random.split(jax.random.key(seed), 4)
    occ_factor = draw_occ_factor(jax.random.fold_in(seeds[3], 71), 0)
    vir_factor = draw_vir_factor(jax.random.fold_in(seeds[3], 71), 0)
    eps_basis = centred(seeds[2], (NAUX, NEPS), NAUX ** -0.5, 0.125, ((0, 8),), jnp.float32)
    return {"occ_factor": occ_factor, "vir_factor": vir_factor, "eps_basis": eps_basis}


highest = lax.Precision.HIGHEST

def cosine_table(length):
    freq_index = jnp.arange(length, dtype=jnp.float32)[:, None]
    time_index = jnp.arange(length, dtype=jnp.float32)[None, :]
    table = jnp.cos(jnp.pi * freq_index * (time_index + 0.5) / length) * jnp.sqrt(2.0 / length)
    return jnp.where(freq_index == 0, table * jnp.sqrt(0.5), table)

def reference(occ_factor, vir_factor, eps_basis):

    def one_time(pair):
        occ_slice, vir_slice = pair
        occ_green = jnp.dot(occ_slice, occ_slice.T, precision=highest, preferred_element_type=jnp.float32)
        vir_green = jnp.dot(vir_slice, vir_slice.T, precision=highest, preferred_element_type=jnp.float32)
        polar = occ_green * vir_green
        return jnp.dot(polar, eps_basis, precision=highest, preferred_element_type=jnp.float32)
    projected = lax.map(one_time, (occ_factor, vir_factor))
    table = cosine_table(NT)
    spectrum = jnp.einsum('kt,tpe->kpe', table, projected, precision=highest)

    def project_left(block):
        return jnp.dot(eps_basis.T, block, precision=highest, preferred_element_type=jnp.float32)
    return lax.map(project_left, spectrum)
```

```python
import functools
import math

import jax
import jax.numpy as jnp
from jax import lax
from jax.experimental import pallas as pl
from jax.experimental.pallas import tpu as pltpu
from jax.sharding import PartitionSpec as P

F32 = jnp.float32
BF16 = jnp.bfloat16
NT_DIMS = (((1,), (1,)), ((), ()))
NN_DIMS = (((1,), (0,)), ((), ()))
TN_DIMS = (((0,), (0,)), ((), ()))
NEXT, OWN, ACROSS, FAR = 0, 1, 2, 3
ROWS = 256
HALF = 128
TILE = 128


def halves_of(x):
    high = x.astype(BF16)
    return high, (x - high.astype(F32)).astype(BF16)


def dot3(lhs, rhs, dims):
    mul = functools.partial(lax.dot_general, dimension_numbers=dims, preferred_element_type=F32)
    return mul(lhs[0], rhs[0]) + (mul(lhs[0], rhs[1]) + mul(lhs[1], rhs[0]))


def green_kernel(
    occ, vir, eps, out, full, high, low, basis, basis_high, basis_low, polar, total, staged, arrived,
    local_sem, basis_send, basis_recv, send, recv, part_send, part_recv,
):
    row, tm = lax.axis_index("row"), lax.axis_index("tm")
    y, z = lax.div(row, 2), lax.rem(row, 2)
    step = 1 - 2 * lax.rem(tm, 2)
    before = {"row": lax.rem(y - step + 4, 4) * 2 + z, "tm": tm}
    across = {"row": y * 2 + 1 - z, "tm": tm}

    barrier = pltpu.get_barrier_semaphore()

    def greet(i, carry):
        pl.semaphore_signal(barrier, inc=1, device_id={"row": lax.rem(row + i, 8), "tm": tm})
        return carry

    lax.fori_loop(1, 8, greet, 0)
    pl.semaphore_wait(barrier, 7)

    def block(slot, chunk=None):
        if chunk is None:
            return pl.ds(slot * ROWS, ROWS)
        return pl.ds(slot * ROWS + chunk * HALF, HALF)

    def send_basis(src, slot, device):
        return pltpu.make_async_remote_copy(
            src, basis.at[block(slot)], basis_send.at[slot], basis_recv.at[slot], device_id=device
        )

    def send_rows(which, chunk, src, slot, device):
        return pltpu.make_async_remote_copy(
            src, full.at[which, block(slot, chunk)],
            send.at[which, slot, chunk], recv.at[which, slot, chunk], device_id=device,
        )

    sources = (occ.at[0], vir.at[0])
    copies = {}
    copies["basis", NEXT] = send_basis(eps, NEXT, before)
    copies["basis", ACROSS] = send_basis(eps, ACROSS, across)
    for chunk in range(2):
        for which in range(2):
            part = sources[which].at[pl.ds(chunk * HALF, HALF)]
            copies[which, NEXT, chunk] = send_rows(which, chunk, part, NEXT, before)
            copies[which, ACROSS, chunk] = send_rows(which, chunk, part, ACROSS, across)
    for copy in copies.values():
        copy.start()

    own = [pltpu.make_async_copy(sources[which], full.at[which, block(OWN)], local_sem.at[which]) for which in range(2)]
    own.append(pltpu.make_async_copy(eps, basis.at[block(OWN)], local_sem.at[2]))
    for copy in own:
        copy.start()
    for copy in own:
        copy.wait()

    def convert(slot, chunk):
        start = slot * ROWS + chunk * HALF

        def body(i, carry):
            rows = pl.ds(start + i * 16, 16)
            for which in range(2):
                high[which, rows], low[which, rows] = halves_of(full[which, rows])
            return carry

        lax.fori_loop(0, HALF // 16, body, 0)

    def convert_basis(slot):
        def body(i, carry):
            rows = pl.ds(slot * ROWS + i * 16, 16)
            basis_high[rows], basis_low[rows] = halves_of(basis[rows])
            return carry

        lax.fori_loop(0, ROWS // 16, body, 0)

    def greens(left, right, width, weight):
        def one(which):
            lhs = (high[which, pl.ds(left, HALF)], low[which, pl.ds(left, HALF)])
            rhs = (high[which, pl.ds(right, width)], low[which, pl.ds(right, width)])
            return dot3(lhs, rhs, NT_DIMS)

        polar[:, pl.ds(right, width)] = weight * (one(0) * one(1))

    def project(left, spans, first):
        term = None
        for start, width in spans:
            rhs = (basis_high[pl.ds(start, width)], basis_low[pl.ds(start, width)])
            new = dot3(halves_of(polar[:, pl.ds(start, width)]), rhs, NN_DIMS)
            term = new if term is None else term + new
        term = halves_of(term)

        def body(i, carry):
            columns = pl.ds(pl.multiple_of(i * 256, 256), 256)
            lhs = (basis_high[pl.ds(left, HALF), columns], basis_low[pl.ds(left, HALF), columns])
            new = dot3(lhs, term, TN_DIMS)
            total[columns] = new if first else total[columns] + new
            return carry

        lax.fori_loop(0, 4, body, 0)

    def at(slot, chunk=0):
        return slot * ROWS + chunk * HALF

    def wait_rows(slot, chunk):
        for which in range(2):
            copies[which, slot, chunk].wait_recv()

    def work(slot, chunk, spans, first=False):
        for start, width, weight in spans:
            greens(at(slot, chunk), start, width, weight)
        project(at(slot, chunk), [span[:2] for span in spans], first)

    convert_basis(OWN)
    for chunk in range(2):
        convert(OWN, chunk)
    work(OWN, 0, [(at(OWN), ROWS, 0.5)], first=True)
    work(OWN, 1, [(at(OWN), ROWS, 0.5)])

    copies["basis", NEXT].wait_recv()
    copies["basis", FAR] = send_basis(basis.at[block(NEXT)], FAR, before)
    copies["basis", FAR].start()
    convert_basis(NEXT)
    for chunk in range(2):
        wait_rows(NEXT, chunk)
        for which in range(2):
            copies[which, FAR, chunk] = send_rows(which, chunk, full.at[which, block(NEXT, chunk)], FAR, before)
            copies[which, FAR, chunk].start()
        convert(NEXT, chunk)
        work(NEXT, chunk, [(at(OWN), ROWS, 1.0)])

    copies["basis", ACROSS].wait_recv()
    convert_basis(ACROSS)
    wait_rows(ACROSS, 0)
    convert(ACROSS, 0)
    work(ACROSS, 0, [(at(NEXT), ROWS, 1.0), (at(OWN), ROWS, 0.5)])
    copies["basis", FAR].wait_recv()
    convert_basis(FAR)
    wait_rows(FAR, 0)
    convert(FAR, 0)
    work(FAR, 0, [(at(OWN), ROWS, 0.5), (at(ACROSS), HALF, 0.5)])
    wait_rows(ACROSS, 1)
    convert(ACROSS, 1)
    work(ACROSS, 1, [(at(NEXT), ROWS, 1.0), (at(OWN), ROWS, 0.5), (at(FAR), HALF, 0.5)])
    wait_rows(FAR, 1)
    convert(FAR, 1)
    work(FAR, 1, [(at(OWN), ROWS, 0.5), (at(ACROSS), ROWS, 0.5)])

    def fold(owner, slot):
        rows = pl.ds(pl.multiple_of(owner * TILE, TILE), TILE)
        for j in range(8):
            tile = pl.ds(j * TILE, TILE)
            staged[slot, tile] = total[rows, tile] + total[tile, rows].T

    def part_copy(owner, i):
        return pltpu.make_async_remote_copy(
            staged.at[i], arrived.at[i], part_send.at[i], part_recv.at[i],
            device_id={"row": owner, "tm": tm},
        )

    def send_part(i, carry):
        owner = lax.rem(row + i, 8)
        fold(owner, i)
        part_copy(owner, i).start()
        return carry

    lax.fori_loop(1, 8, send_part, 0)
    fold(row, 0)

    def take_part(i, carry):
        part_copy(row, i).wait_recv()
        return carry

    lax.fori_loop(1, 8, take_part, 0)

    def add(i, carry):
        rows = pl.ds(i * 64, 64)
        value = staged[0, rows]
        for j in range(1, 8):
            value = value + arrived[j, rows]
        out[rows] = value
        return carry

    lax.fori_loop(0, 16, add, 0)

    for copy in copies.values():
        copy.wait_send()

    def drain(i, carry):
        part_copy(row, i).wait_send()
        return carry

    lax.fori_loop(1, 8, drain, 0)


def green_sums(occ, vir, eps):
    dma = pltpu.SemaphoreType.DMA
    return pl.pallas_call(
        green_kernel,
        out_shape=jax.ShapeDtypeStruct((1024, TILE), F32),
        in_specs=[pl.BlockSpec(memory_space=pl.ANY)] * 3,
        out_specs=pl.BlockSpec(memory_space=pltpu.VMEM),
        scratch_shapes=[
            pltpu.VMEM((2, 4 * ROWS, 2048), F32),
            pltpu.VMEM((2, 4 * ROWS, 2048), BF16),
            pltpu.VMEM((2, 4 * ROWS, 2048), BF16),
            pltpu.VMEM((4 * ROWS, 1024), F32),
            pltpu.VMEM((4 * ROWS, 1024), BF16),
            pltpu.VMEM((4 * ROWS, 1024), BF16),
            pltpu.VMEM((HALF, 4 * ROWS), F32),
            pltpu.VMEM((1024, 1024), F32),
            pltpu.VMEM((8, 1024, TILE), F32),
            pltpu.VMEM((8, 1024, TILE), F32),
            dma((3,)), dma((4,)), dma((4,)), dma((2, 4, 2)), dma((2, 4, 2)), dma((8,)), dma((8,)),
        ],
        compiler_params=pltpu.CompilerParams(
            collective_id=0, has_side_effects=True, vmem_limit_bytes=62 << 20
        ),
        cost_estimate=pl.CostEstimate(flops=20 * 10**9, bytes_accessed=20 << 20, transcendentals=0),
        name="green_sums",
    )(occ, vir, eps)


def cosine(freq, time):
    scale = math.sqrt((1.0 if freq == 0 else 2.0) / 32)
    return scale * math.cos(math.pi * freq * (time + 0.5) / 32)


def cosine_kernel(
    block, out, paired, times, freqs, gathered, final,
    core_send, core_recv, chip_send, chip_recv, back_send, back_recv, end_send, end_recv,
):
    row, tm = lax.axis_index("row"), lax.axis_index("tm")
    chip, core = lax.div(tm, 2), lax.rem(tm, 2)
    partner = {"row": row, "tm": chip * 2 + 1 - core}

    def other(i):
        return lax.rem(lax.div(chip, 4) + lax.div(i, 4), 4) * 4 + lax.rem(lax.rem(chip, 4) + lax.rem(i, 4), 4)

    barrier = pltpu.get_barrier_semaphore()

    def greet(i, carry):
        pl.semaphore_signal(barrier, inc=1, device_id={"row": row, "tm": other(i) * 2 + core})
        return carry

    lax.fori_loop(1, 16, greet, 0)
    pl.semaphore_signal(barrier, inc=1, device_id=partner)
    pl.semaphore_wait(barrier, 16)

    swap = pltpu.make_async_remote_copy(
        block.at[pl.ds(pl.multiple_of((1 - core) * 512, 512), 512)], paired.at[core],
        core_send, core_recv, device_id=partner,
    )
    swap.start()
    paired[core] = block[pl.ds(pl.multiple_of(core * 512, 512), 512)]
    swap.wait()

    def spread(i, carry):
        target = other(i)
        pltpu.make_async_remote_copy(
            paired.at[:, pl.ds(pl.multiple_of(target * 32, 32), 32)], times.at[chip],
            chip_send, chip_recv, device_id={"row": row, "tm": target * 2 + core},
        ).start()
        return carry

    lax.fori_loop(1, 16, spread, 0)
    times[chip] = paired[:, pl.ds(pl.multiple_of(chip * 32, 32), 32)]
    pltpu.make_async_copy(times.at[pl.ds(0, 15)], times.at[pl.ds(0, 15)], chip_recv).wait()

    def transform(i, carry):
        rows = pl.ds(pl.multiple_of(i * 8, 8), 8)
        at = [times[t // 2, t % 2, rows] for t in range(32)]
        mixed = ([at[t] + at[31 - t] for t in range(16)], [at[t] - at[31 - t] for t in range(16)])
        for freq in range(32):
            value = None
            for t in range(16):
                term = cosine(freq, t) * mixed[freq % 2][t]
                value = term if value is None else value + term
            freqs[freq // 2, freq % 2, rows] = value
        return carry

    lax.fori_loop(0, 4, transform, 0)

    def give(i, carry):
        target = other(i)
        pltpu.make_async_remote_copy(
            freqs.at[target], gathered.at[chip],
            back_send, back_recv, device_id={"row": row, "tm": target * 2 + core},
        ).start()
        return carry

    lax.fori_loop(1, 16, give, 0)
    gathered[chip] = freqs[chip]
    pltpu.make_async_copy(gathered.at[pl.ds(0, 15)], gathered.at[pl.ds(0, 15)], back_recv).wait()

    last = pltpu.make_async_remote_copy(
        gathered.at[:, 1 - core], final.at[core], end_send, end_recv, device_id=partner
    )
    last.start()
    final[core] = gathered[:, core]
    last.wait()
    for j in range(8):
        for part in range(4):
            out[0, part * 32:(part + 1) * 32, j * TILE:(j + 1) * TILE] = final[j // 4, (j % 4) * 4 + part]

    pltpu.make_async_copy(times.at[pl.ds(0, 15)], times.at[pl.ds(0, 15)], chip_send).wait()
    pltpu.make_async_copy(times.at[pl.ds(0, 15)], times.at[pl.ds(0, 15)], back_send).wait()


def cosine_sums(block):
    dma = pltpu.SemaphoreType.DMA
    return pl.pallas_call(
        cosine_kernel,
        out_shape=jax.ShapeDtypeStruct((1, TILE, 1024), F32),
        in_specs=[pl.BlockSpec(memory_space=pltpu.VMEM)],
        out_specs=pl.BlockSpec(memory_space=pltpu.VMEM),
        scratch_shapes=[
            pltpu.VMEM((2, 512, TILE), F32),
            pltpu.VMEM((16, 2, 32, TILE), F32),
            pltpu.VMEM((16, 2, 32, TILE), F32),
            pltpu.VMEM((16, 2, 32, TILE), F32),
            pltpu.VMEM((2, 16, 32, TILE), F32),
            dma, dma, dma, dma, dma, dma, dma, dma,
        ],
        compiler_params=pltpu.CompilerParams(
            collective_id=1, has_side_effects=True, vmem_limit_bytes=16 << 20
        ),
        cost_estimate=pl.CostEstimate(flops=10**7, bytes_accessed=1 << 20, transcendentals=0),
        name="cosine_sums",
    )(block)


def on_device(occ_factor, vir_factor, eps_basis):
    return cosine_sums(green_sums(occ_factor, vir_factor, eps_basis))


def solution(mesh):
    placed = (P("tm", "row", None), P("tm", "row", None), P("row", None))
    return jax.shard_map(
        on_device, mesh=mesh, in_specs=placed, out_specs=P("tm", "row", None), check_vma=False
    )
```

```python
import functools
import math

import jax
import jax.numpy as jnp
from jax import lax
from jax.experimental import pallas as pl
from jax.experimental.pallas import tpu as pltpu
from jax.sharding import PartitionSpec as P

F32 = jnp.float32
BF16 = jnp.bfloat16
NT_DIMS = (((1,), (1,)), ((), ()))
NN_DIMS = (((1,), (0,)), ((), ()))
TN_DIMS = (((0,), (0,)), ((), ()))
NEXT, OWN, ACROSS, FAR = 0, 1, 2, 3
ROWS = 256
HALF = 128
TILE = 128
QUARTER = 64
KEPT = 4 * TILE + 64
SHARE = KEPT // 2
MAIN = 256


def halves_of(x):
    high = x.astype(BF16)
    return high, (x - high.astype(F32)).astype(BF16)


def dot3(lhs, rhs, dims):
    mul = functools.partial(lax.dot_general, dimension_numbers=dims, preferred_element_type=F32)
    return mul(lhs[0], rhs[0]) + (mul(lhs[0], rhs[1]) + mul(lhs[1], rhs[0]))


def green_kernel(
    occ, vir, eps, out, full, high, low, basis, basis_high, basis_low, polar, total, turned, staged, arrived,
    local_sem, basis_send, basis_recv, share_send, share_recv, send, recv, part_send, part_recv,
):
    row, tm = lax.axis_index("row"), lax.axis_index("tm")
    y, z = lax.div(row, 2), lax.rem(row, 2)
    step = 1 - 2 * lax.rem(tm, 2)
    before = {"row": lax.rem(y - step + 4, 4) * 2 + z, "tm": tm}
    across = {"row": y * 2 + 1 - z, "tm": tm}
    x = lax.div(tm, 8)
    beside = [{"row": row, "tm": lax.rem(tm + 8 * i, 32)} for i in range(4)]

    barrier = pltpu.get_barrier_semaphore()

    def greet(i, carry):
        pl.semaphore_signal(barrier, inc=1, device_id={"row": lax.rem(row + i, 8), "tm": tm})
        return carry

    lax.fori_loop(1, 8, greet, 0)
    for i in range(1, 4):
        pl.semaphore_signal(barrier, inc=1, device_id=beside[i])
    pl.semaphore_wait(barrier, 10)

    def block(slot, chunk=None):
        if chunk is None:
            return pl.ds(slot * ROWS, ROWS)
        return pl.ds(slot * ROWS + chunk * HALF, HALF)

    def quarter(slot, of):
        return pl.ds(pl.multiple_of(slot * ROWS + of * QUARTER, QUARTER), QUARTER)

    def send_basis(src, slot, device):
        return pltpu.make_async_remote_copy(
            src, basis.at[quarter(slot, x)], basis_send.at[slot], basis_recv.at[slot], device_id=device
        )

    def share_basis(slot):
        copies["basis", slot].wait_recv()
        part = basis.at[quarter(slot, x)]
        for i in range(1, 4):
            copies["share", slot, i] = pltpu.make_async_remote_copy(
                part, part, share_send.at[slot, i], share_recv.at[slot, i], device_id=beside[i]
            )
            copies["share", slot, i].start()

    def take_basis(slot):
        for i in range(1, 4):
            copies["share", slot, i].wait_recv()
        convert_basis(slot)

    def send_rows(which, chunk, src, slot, device):
        return pltpu.make_async_remote_copy(
            src, full.at[which, block(slot, chunk)],
            send.at[which, slot, chunk], recv.at[which, slot, chunk], device_id=device,
        )

    sources = (occ.at[0], vir.at[0])
    copies = {}
    copies["basis", NEXT] = send_basis(eps.at[quarter(0, x)], NEXT, before)
    copies["basis", ACROSS] = send_basis(eps.at[quarter(0, x)], ACROSS, across)
    for chunk in range(2):
        for which in range(2):
            part = sources[which].at[pl.ds(chunk * HALF, HALF)]
            copies[which, NEXT, chunk] = send_rows(which, chunk, part, NEXT, before)
            copies[which, ACROSS, chunk] = send_rows(which, chunk, part, ACROSS, across)
    for copy in copies.values():
        copy.start()

    own = [pltpu.make_async_copy(sources[which], full.at[which, block(OWN)], local_sem.at[which]) for which in range(2)]
    own.append(pltpu.make_async_copy(eps, basis.at[block(OWN)], local_sem.at[2]))
    for copy in own:
        copy.start()
    for copy in own:
        copy.wait()

    def convert(slot, chunk):
        start = slot * ROWS + chunk * HALF

        def body(i, carry):
            rows = pl.ds(start + i * 16, 16)
            for which in range(2):
                high[which, rows], low[which, rows] = halves_of(full[which, rows])
            return carry

        lax.fori_loop(0, HALF // 16, body, 0)

    def convert_basis(slot):
        def body(i, carry):
            rows = pl.ds(slot * ROWS + i * 16, 16)
            basis_high[rows], basis_low[rows] = halves_of(basis[rows])
            return carry

        lax.fori_loop(0, ROWS // 16, body, 0)

    def greens(left, right, width, weight):
        def one(which):
            lhs = (high[which, pl.ds(left, HALF)], low[which, pl.ds(left, HALF)])
            rhs = (high[which, pl.ds(right, width)], low[which, pl.ds(right, width)])
            return dot3(lhs, rhs, NT_DIMS)

        polar[:, pl.ds(right, width)] = weight * (one(0) * one(1))

    def project(left, spans, first):
        term = None
        for start, width in spans:
            rhs = (basis_high[pl.ds(start, width)], basis_low[pl.ds(start, width)])
            new = dot3(halves_of(polar[:, pl.ds(start, width)]), rhs, NN_DIMS)
            term = new if term is None else term + new
        term = halves_of(term)

        def body(i, carry):
            columns = pl.ds(pl.multiple_of(i * 256, 256), 256)
            lhs = (basis_high[pl.ds(left, HALF), columns], basis_low[pl.ds(left, HALF), columns])
            new = dot3(lhs, term, TN_DIMS)
            total[columns] = new if first else total[columns] + new
            return carry

        lax.fori_loop(0, 4, body, 0)

    def at(slot, chunk=0):
        return slot * ROWS + chunk * HALF

    def wait_rows(slot, chunk):
        for which in range(2):
            copies[which, slot, chunk].wait_recv()

    def work(slot, chunk, spans, first=False):
        for start, width, weight in spans:
            greens(at(slot, chunk), start, width, weight)
        project(at(slot, chunk), [span[:2] for span in spans], first)

    convert_basis(OWN)
    share_basis(NEXT)
    copies["basis", FAR] = send_basis(basis.at[quarter(NEXT, x)], FAR, before)
    copies["basis", FAR].start()
    share_basis(ACROSS)
    for chunk in range(2):
        convert(OWN, chunk)
    work(OWN, 0, [(at(OWN), ROWS, 0.5)], first=True)
    work(OWN, 1, [(at(OWN), ROWS, 0.5)])
    share_basis(FAR)
    take_basis(NEXT)
    take_basis(ACROSS)
    take_basis(FAR)

    for chunk in range(2):
        wait_rows(NEXT, chunk)
        for which in range(2):
            copies[which, FAR, chunk] = send_rows(which, chunk, full.at[which, block(NEXT, chunk)], FAR, before)
            copies[which, FAR, chunk].start()
        convert(NEXT, chunk)
        work(NEXT, chunk, [(at(OWN), ROWS, 1.0)])

    wait_rows(ACROSS, 0)
    convert(ACROSS, 0)
    work(ACROSS, 0, [(at(NEXT), ROWS, 1.0), (at(OWN), ROWS, 0.5)])
    wait_rows(FAR, 0)
    convert(FAR, 0)
    work(FAR, 0, [(at(OWN), ROWS, 0.5), (at(ACROSS), HALF, 0.5)])
    wait_rows(ACROSS, 1)
    convert(ACROSS, 1)
    work(ACROSS, 1, [(at(NEXT), ROWS, 1.0), (at(OWN), ROWS, 0.5), (at(FAR), HALF, 0.5)])
    wait_rows(FAR, 1)
    convert(FAR, 1)
    work(FAR, 1, [(at(OWN), ROWS, 0.5), (at(ACROSS), ROWS, 0.5)])

    def fold(owner, slot):
        def span(j):
            return pl.ds(pl.multiple_of(j * TILE, TILE), TILE)

        rows = span(owner)
        for d in range(4):
            tile = span(lax.rem(owner + d, 8))
            staged[slot, d * TILE:(d + 1) * TILE] = total[rows, tile] + total[tile, rows].T
        low_tile, upper = lax.rem(owner, 4), lax.div(owner, 4)
        turned[...] = total[span(low_tile + 4), span(low_tile)].T
        half = pl.ds(pl.multiple_of(low_tile * TILE + upper * 64, 64), 64)
        staged[slot, 4 * TILE:KEPT] = (
            total[half, span(low_tile + 4)] + turned[pl.ds(pl.multiple_of(upper * 64, 64), 64)]
        )

    def part_copy(owner, i):
        return pltpu.make_async_remote_copy(
            staged.at[i], arrived.at[i], part_send.at[i], part_recv.at[i],
            device_id={"row": owner, "tm": tm},
        )

    def send_part(i, carry):
        owner = lax.rem(row + i, 8)
        fold(owner, i)
        part_copy(owner, i).start()
        return carry

    lax.fori_loop(1, 8, send_part, 0)
    fold(row, 0)

    def take_part(i, carry):
        part_copy(row, i).wait_recv()
        return carry

    lax.fori_loop(1, 8, take_part, 0)

    def add(i, carry):
        rows = pl.ds(i * 64, 64)
        value = staged[0, rows]
        for j in range(1, 8):
            value = value + arrived[j, rows]
        out[rows] = value
        return carry

    lax.fori_loop(0, KEPT // 64, add, 0)

    for copy in copies.values():
        copy.wait_send()

    def drain(i, carry):
        part_copy(row, i).wait_send()
        return carry

    lax.fori_loop(1, 8, drain, 0)


def green_sums(occ, vir, eps):
    dma = pltpu.SemaphoreType.DMA
    return pl.pallas_call(
        green_kernel,
        out_shape=jax.ShapeDtypeStruct((KEPT, TILE), F32),
        in_specs=[pl.BlockSpec(memory_space=pl.ANY)] * 3,
        out_specs=pl.BlockSpec(memory_space=pltpu.VMEM),
        scratch_shapes=[
            pltpu.VMEM((2, 4 * ROWS, 2048), F32),
            pltpu.VMEM((2, 4 * ROWS, 2048), BF16),
            pltpu.VMEM((2, 4 * ROWS, 2048), BF16),
            pltpu.VMEM((4 * ROWS, 1024), F32),
            pltpu.VMEM((4 * ROWS, 1024), BF16),
            pltpu.VMEM((4 * ROWS, 1024), BF16),
            pltpu.VMEM((HALF, 4 * ROWS), F32),
            pltpu.VMEM((1024, 1024), F32),
            pltpu.VMEM((TILE, TILE), F32),
            pltpu.VMEM((8, KEPT, TILE), F32),
            pltpu.VMEM((8, KEPT, TILE), F32),
            dma((3,)), dma((4,)), dma((4,)), dma((4, 4)), dma((4, 4)), dma((2, 4, 2)), dma((2, 4, 2)), dma((8,)), dma((8,)),
        ],
        compiler_params=pltpu.CompilerParams(
            collective_id=0, has_side_effects=True, vmem_limit_bytes=62 << 20
        ),
        cost_estimate=pl.CostEstimate(flops=20 * 10**9, bytes_accessed=20 << 20, transcendentals=0),
        name="green_sums",
    )(occ, vir, eps)


def cosine(freq, time):
    scale = math.sqrt((1.0 if freq == 0 else 2.0) / 32)
    return scale * math.cos(math.pi * freq * (time + 0.5) / 32)


def cosine_kernel(
    block, out, paired, times, times_more, freqs, freqs_more, gathered, gathered_more, final, final_more,
    flat, mirror, mirror_half, joined,
    swap_send, swap_recv, chip_send, chip_recv, more_send, more_recv, back_send, back_recv,
    back_more_send, back_more_recv, end_send, end_recv, mirror_send, mirror_recv,
):
    row, tm = lax.axis_index("row"), lax.axis_index("tm")
    chip, core = lax.div(tm, 2), lax.rem(tm, 2)
    partner = {"row": row, "tm": chip * 2 + 1 - core}
    has_more = lax.rem(chip, 5) == 0

    def other(i):
        return lax.rem(lax.div(chip, 4) + lax.div(i, 4), 4) * 4 + lax.rem(lax.rem(chip, 4) + lax.rem(i, 4), 4)

    def device(target):
        return {"row": row, "tm": target * 2 + core}

    def aligned(start, size):
        return pl.ds(pl.multiple_of(start, size), size)

    barrier = pltpu.get_barrier_semaphore()

    def greet(i, carry):
        pl.semaphore_signal(barrier, inc=1, device_id=device(other(i)))
        return carry

    def greet_row(i, carry):
        pl.semaphore_signal(barrier, inc=1, device_id={"row": lax.rem(row + i, 8), "tm": tm})
        return carry

    lax.fori_loop(1, 16, greet, 0)
    lax.fori_loop(1, 8, greet_row, 0)
    pl.semaphore_signal(barrier, inc=1, device_id=partner)
    pl.semaphore_wait(barrier, 23)

    swap = pltpu.make_async_remote_copy(
        block.at[aligned((1 - core) * SHARE, SHARE)], paired.at[core], swap_send, swap_recv, device_id=partner,
    )
    swap.start()
    paired[core] = block[aligned(core * SHARE, SHARE)]
    swap.wait()

    def more_copy(e):
        return pltpu.make_async_remote_copy(
            paired.at[:, MAIN + e * 8:MAIN + e * 8 + 8], times_more.at[chip],
            more_send.at[e], more_recv, device_id=device(5 * e),
        )

    def spread(i, carry):
        target = other(i)
        pltpu.make_async_remote_copy(
            paired.at[:, aligned(target * 16, 16)], times.at[chip],
            chip_send, chip_recv, device_id=device(target),
        ).start()
        return carry

    lax.fori_loop(1, 16, spread, 0)
    for e in range(4):
        @pl.when(chip != 5 * e)
        def _():
            more_copy(e).start()

        @pl.when(chip == 5 * e)
        def _():
            times_more[chip] = paired[:, MAIN + e * 8:MAIN + e * 8 + 8]
    times[chip] = paired[:, aligned(chip * 16, 16)]
    pltpu.make_async_copy(times.at[pl.ds(0, 15)], times.at[pl.ds(0, 15)], chip_recv).wait()

    def transform(source, result, rows):
        at = [source[t // 2, t % 2, rows] for t in range(32)]
        mixed = ([at[t] + at[31 - t] for t in range(16)], [at[t] - at[31 - t] for t in range(16)])
        for freq in range(32):
            value = None
            for t in range(16):
                term = cosine(freq, t) * mixed[freq % 2][t]
                value = term if value is None else value + term
            result[freq // 2, freq % 2, rows] = value

    def transform_main(i, carry):
        transform(times, freqs, aligned(i * 8, 8))
        return carry

    lax.fori_loop(0, 2, transform_main, 0)

    def give(i, carry):
        target = other(i)
        pltpu.make_async_remote_copy(
            freqs.at[target], gathered.at[chip], back_send, back_recv, device_id=device(target),
        ).start()
        return carry

    lax.fori_loop(1, 16, give, 0)

    def back_more_copy(target, e):
        return pltpu.make_async_remote_copy(
            freqs_more.at[target], gathered_more.at[e],
            back_more_send, back_more_recv.at[e], device_id=device(target),
        )

    @pl.when(has_more)
    def _():
        pltpu.make_async_copy(times_more.at[pl.ds(0, 15)], times_more.at[pl.ds(0, 15)], more_recv).wait()
        transform(times_more, freqs_more, pl.ds(0, 8))

        def give_more(i, carry):
            back_more_copy(other(i), lax.div(chip, 5)).start()
            return carry

        lax.fori_loop(1, 16, give_more, 0)
        gathered_more[lax.div(chip, 5)] = freqs_more[chip]

    gathered[chip] = freqs[chip]
    pltpu.make_async_copy(gathered.at[pl.ds(0, 15)], gathered.at[pl.ds(0, 15)], back_recv).wait()
    last = pltpu.make_async_remote_copy(
        gathered.at[:, 1 - core], final.at[core], end_send.at[0], end_recv.at[0], device_id=partner
    )
    last.start()
    for e in range(4):
        @pl.when(chip != 5 * e)
        def _():
            back_more_copy(chip, e).wait_recv()
    last_more = pltpu.make_async_remote_copy(
        gathered_more.at[:, 1 - core], final_more.at[core], end_send.at[1], end_recv.at[1], device_id=partner
    )
    last_more.start()
    final[core] = gathered[:, core]
    final_more[core] = gathered_more[:, core]
    last.wait()
    last_more.wait()
    for c in range(2):
        for p in range(16):
            flat[c * SHARE + p * 16:c * SHARE + p * 16 + 16] = final[c, p]
        for e in range(4):
            flat[c * SHARE + MAIN + e * 8:c * SHARE + MAIN + e * 8 + 8] = final_more[c, e]

    mirrors = []
    for d in range(1, 5):
        part, to = (pl.ds(d * TILE, TILE), mirror.at[d - 1]) if d < 4 else (pl.ds(4 * TILE, 64), mirror_half)
        mirrors.append(pltpu.make_async_remote_copy(
            flat.at[part], to, mirror_send.at[d - 1], mirror_recv.at[d - 1],
            device_id={"row": lax.rem(row + d, 8), "tm": tm},
        ))
        mirrors[-1].start()

    def columns(j):
        return aligned(lax.rem(j, 8) * TILE, TILE)

    for d in range(4):
        out[0, :, columns(row + d)] = flat[d * TILE:(d + 1) * TILE]
    for d in range(1, 4):
        mirrors[d - 1].wait_recv()
        out[0, :, columns(row + 8 - d)] = mirror[d - 1].T
    mirrors[3].wait_recv()
    upper = lax.div(row, 4)
    joined[aligned(upper * 64, 64)] = flat[4 * TILE:KEPT]
    joined[aligned((1 - upper) * 64, 64)] = mirror_half[...]

    @pl.when(upper == 0)
    def _():
        out[0, :, columns(row + 4)] = joined[...]

    @pl.when(upper == 1)
    def _():
        out[0, :, columns(row + 4)] = joined[...].T

    for copy in mirrors:
        copy.wait_send()
    pltpu.make_async_copy(times.at[pl.ds(0, 15)], times.at[pl.ds(0, 15)], chip_send).wait()
    pltpu.make_async_copy(times.at[pl.ds(0, 15)], times.at[pl.ds(0, 15)], back_send).wait()
    for e in range(4):
        @pl.when(chip != 5 * e)
        def _():
            more_copy(e).wait_send()

    @pl.when(has_more)
    def _():
        pltpu.make_async_copy(times_more.at[pl.ds(0, 15)], times_more.at[pl.ds(0, 15)], back_more_send).wait()


def cosine_sums(block):
    dma = pltpu.SemaphoreType.DMA
    main = pltpu.VMEM((16, 2, 16, TILE), F32)
    more = pltpu.VMEM((16, 2, 8, TILE), F32)
    return pl.pallas_call(
        cosine_kernel,
        out_shape=jax.ShapeDtypeStruct((1, TILE, 1024), F32),
        in_specs=[pl.BlockSpec(memory_space=pltpu.VMEM)],
        out_specs=pl.BlockSpec(memory_space=pltpu.VMEM),
        scratch_shapes=[
            pltpu.VMEM((2, SHARE, TILE), F32),
            main, more, main, more, main,
            pltpu.VMEM((4, 2, 8, TILE), F32),
            pltpu.VMEM((2, 16, 16, TILE), F32),
            pltpu.VMEM((2, 4, 8, TILE), F32),
            pltpu.VMEM((KEPT, TILE), F32),
            pltpu.VMEM((3, TILE, TILE), F32),
            pltpu.VMEM((64, TILE), F32),
            pltpu.VMEM((TILE, TILE), F32),
            dma, dma, dma, dma, dma((4,)), dma, dma, dma, dma, dma((4,)), dma((2,)), dma((2,)), dma((4,)), dma((4,)),
        ],
        compiler_params=pltpu.CompilerParams(
            collective_id=1, has_side_effects=True, vmem_limit_bytes=16 << 20
        ),
        cost_estimate=pl.CostEstimate(flops=10**7, bytes_accessed=1 << 20, transcendentals=0),
        name="cosine_sums",
    )(block)


def on_device(occ_factor, vir_factor, eps_basis):
    return cosine_sums(green_sums(occ_factor, vir_factor, eps_basis))


def solution(mesh):
    placed = (P("tm", "row", None), P("tm", "row", None), P("row", None))
    return jax.shard_map(
        on_device, mesh=mesh, in_specs=placed, out_specs=P("tm", "row", None), check_vma=False
    )
```

```python
import functools
import math

import jax
import jax.numpy as jnp
from jax import lax
from jax.experimental import pallas as pl
from jax.experimental.pallas import tpu as pltpu
from jax.sharding import PartitionSpec as P

F32 = jnp.float32
BF16 = jnp.bfloat16
NT_DIMS = (((1,), (1,)), ((), ()))
NN_DIMS = (((1,), (0,)), ((), ()))
TN_DIMS = (((0,), (0,)), ((), ()))
NEXT, OWN, ACROSS, FAR = 0, 1, 2, 3
ROWS = 256
PARTS = ((0, 128), (128, 128))
TILE = 128
QUARTER = 64
KEPT = 4 * TILE + 64
SHARE = KEPT // 2
MAIN = 256
GREEN_SCRATCH = 20


def ring_place(row):
    y, z = lax.div(row, 2), lax.rem(row, 2)
    return y + z * (7 - 2 * y)


def ring_row(place):
    place = lax.rem(place, 8)
    z = lax.div(place, 4)
    return (place + z * (7 - 2 * place)) * 2 + z


def halves_of(x):
    high = x.astype(BF16)
    return high, (x - high.astype(F32)).astype(BF16)


def dot3(lhs, rhs, dims):
    mul = functools.partial(lax.dot_general, dimension_numbers=dims, preferred_element_type=F32)
    return mul(lhs[0], rhs[0]) + (mul(lhs[0], rhs[1]) + mul(lhs[1], rhs[0]))


def green_kernel(
    occ, vir, eps, out, full, high, low, basis, basis_high, basis_low, polar, total, turned, staged, arrived,
    local_sem, basis_send, basis_recv, share_send, share_recv, send, recv, part_send, part_recv,
):
    row, tm = lax.axis_index("row"), lax.axis_index("tm")
    y, z = lax.div(row, 2), lax.rem(row, 2)
    step = 1 - 2 * lax.rem(tm, 2)
    before = {"row": lax.rem(y - step + 4, 4) * 2 + z, "tm": tm}
    across = {"row": y * 2 + 1 - z, "tm": tm}
    x = lax.div(tm, 8)
    beside = [{"row": row, "tm": lax.rem(tm + 8 * i, 32)} for i in range(4)]

    def block(slot, chunk=None):
        if chunk is None:
            return pl.ds(slot * ROWS, ROWS)
        return pl.ds(slot * ROWS + PARTS[chunk][0], PARTS[chunk][1])

    def quarter(slot, of):
        return pl.ds(pl.multiple_of(slot * ROWS + of * QUARTER, QUARTER), QUARTER)

    def send_basis(src, slot, device):
        return pltpu.make_async_remote_copy(
            src, basis.at[quarter(slot, x)], basis_send.at[slot], basis_recv.at[slot], device_id=device
        )

    def share_basis(slot):
        copies["basis", slot].wait_recv()
        part = basis.at[quarter(slot, x)]
        for i in range(1, 4):
            copies["share", slot, i] = pltpu.make_async_remote_copy(
                part, part, share_send.at[slot, i], share_recv.at[slot, i], device_id=beside[i]
            )
            copies["share", slot, i].start()

    def take_basis(slot):
        for i in range(1, 4):
            copies["share", slot, i].wait_recv()
        convert_basis(slot)

    def send_rows(which, chunk, src, slot, device):
        return pltpu.make_async_remote_copy(
            src, full.at[which, block(slot, chunk)],
            send.at[which, slot, chunk], recv.at[which, slot, chunk], device_id=device,
        )

    sources = (occ.at[0], vir.at[0])
    copies = {}
    copies["basis", NEXT] = send_basis(eps.at[quarter(0, x)], NEXT, before)
    copies["basis", ACROSS] = send_basis(eps.at[quarter(0, x)], ACROSS, across)
    for chunk in range(len(PARTS)):
        for which in range(2):
            part = sources[which].at[pl.ds(*PARTS[chunk])]
            copies[which, NEXT, chunk] = send_rows(which, chunk, part, NEXT, before)
            copies[which, ACROSS, chunk] = send_rows(which, chunk, part, ACROSS, across)
    for copy in copies.values():
        copy.start()

    own = [pltpu.make_async_copy(sources[which], full.at[which, block(OWN)], local_sem.at[which]) for which in range(2)]
    own.append(pltpu.make_async_copy(eps, basis.at[block(OWN)], local_sem.at[2]))
    for copy in own:
        copy.start()
    for copy in own:
        copy.wait()

    def convert(slot, first, size):
        start = slot * ROWS + first

        def body(i, carry):
            rows = pl.ds(start + i * 16, 16)
            for which in range(2):
                high[which, rows], low[which, rows] = halves_of(full[which, rows])
            return carry

        lax.fori_loop(0, size // 16, body, 0)

    def convert_basis(slot):
        def body(i, carry):
            rows = pl.ds(slot * ROWS + i * 16, 16)
            basis_high[rows], basis_low[rows] = halves_of(basis[rows])
            return carry

        lax.fori_loop(0, ROWS // 16, body, 0)

    def greens(left, size, right, width, weight):
        def one(which):
            lhs = (high[which, pl.ds(left, size)], low[which, pl.ds(left, size)])
            rhs = (high[which, pl.ds(right, width)], low[which, pl.ds(right, width)])
            return dot3(lhs, rhs, NT_DIMS)

        polar[0:size, pl.ds(right, width)] = weight * (one(0) * one(1))

    def project(left, size, spans, first):
        term = None
        for start, width in spans:
            rhs = (basis_high[pl.ds(start, width)], basis_low[pl.ds(start, width)])
            new = dot3(halves_of(polar[0:size, pl.ds(start, width)]), rhs, NN_DIMS)
            term = new if term is None else term + new
        term = halves_of(term)

        def body(i, carry):
            columns = pl.ds(pl.multiple_of(i * 256, 256), 256)
            lhs = (basis_high[pl.ds(left, size), columns], basis_low[pl.ds(left, size), columns])
            new = dot3(lhs, term, TN_DIMS)
            total[columns] = new if first else total[columns] + new
            return carry

        lax.fori_loop(0, 4, body, 0)

    def at(slot, first=0):
        return slot * ROWS + first

    def wait_rows(slot, chunk):
        for which in range(2):
            copies[which, slot, chunk].wait_recv()

    def work(slot, first, size, spans, opening=False):
        for start, width, weight in spans:
            greens(at(slot, first), size, start, width, weight)
        project(at(slot, first), size, [span[:2] for span in spans], opening)

    convert_basis(OWN)
    share_basis(NEXT)
    copies["basis", FAR] = send_basis(basis.at[quarter(NEXT, x)], FAR, before)
    copies["basis", FAR].start()
    share_basis(ACROSS)
    convert(OWN, 0, ROWS)
    work(OWN, 0, 128, [(at(OWN), ROWS, 0.5)], opening=True)
    work(OWN, 128, 128, [(at(OWN), ROWS, 0.5)])
    for chunk in range(len(PARTS)):
        wait_rows(NEXT, chunk)
        for which in range(2):
            copies[which, FAR, chunk] = send_rows(which, chunk, full.at[which, block(NEXT, chunk)], FAR, before)
            copies[which, FAR, chunk].start()
    share_basis(FAR)
    take_basis(NEXT)
    convert(NEXT, 0, ROWS)
    work(NEXT, 0, 128, [(at(OWN), ROWS, 1.0)])
    work(NEXT, 128, 128, [(at(OWN), ROWS, 1.0)])

    take_basis(ACROSS)
    have = {ACROSS: 0, FAR: 0}
    for chunk in range(len(PARTS)):
        for slot, spans, mate in (
            (ACROSS, [(at(NEXT), ROWS, 1.0), (at(OWN), ROWS, 0.5)], FAR),
            (FAR, [(at(OWN), ROWS, 0.5)], ACROSS),
        ):
            if slot == FAR and chunk == 0:
                take_basis(FAR)
            wait_rows(slot, chunk)
            convert(slot, *PARTS[chunk])
            more = [(at(mate), have[mate], 0.5)] if have[mate] else []
            work(slot, *PARTS[chunk], spans + more)
            have[slot] += PARTS[chunk][1]

    def fold(owner, slot):
        def span(j):
            return pl.ds(pl.multiple_of(j * TILE, TILE), TILE)

        rows = span(owner)
        place = ring_place(owner)
        for d in range(4):
            tile = span(ring_row(place + d))
            staged[slot, d * TILE:(d + 1) * TILE] = total[rows, tile] + total[tile, rows].T
        upper = lax.div(place, 4)
        low_tile, high_tile = ring_row(lax.rem(place, 4)), ring_row(lax.rem(place, 4) + 4)
        turned[...] = total[span(high_tile), span(low_tile)].T
        half = pl.ds(pl.multiple_of(low_tile * TILE + upper * 64, 64), 64)
        staged[slot, 4 * TILE:KEPT] = (
            total[half, span(high_tile)] + turned[pl.ds(pl.multiple_of(upper * 64, 64), 64)]
        )

    def part_copy(owner, i):
        return pltpu.make_async_remote_copy(
            staged.at[i], arrived.at[i], part_send.at[i], part_recv.at[i],
            device_id={"row": owner, "tm": tm},
        )

    def send_part(i, carry):
        owner = lax.rem(row + i, 8)
        fold(owner, i)
        part_copy(owner, i).start()
        return carry

    lax.fori_loop(1, 8, send_part, 0)
    fold(row, 0)

    def take_part(i, carry):
        part_copy(row, i).wait_recv()
        return carry

    lax.fori_loop(1, 8, take_part, 0)

    def add(i, carry):
        rows = pl.ds(i * 64, 64)
        value = staged[0, rows]
        for j in range(1, 8):
            value = value + arrived[j, rows]
        out[rows] = value
        return carry

    lax.fori_loop(0, KEPT // 64, add, 0)

    def finish():
        for copy in copies.values():
            copy.wait_send()

        def drain(i, carry):
            part_copy(row, i).wait_send()
            return carry

        lax.fori_loop(1, 8, drain, 0)

    return finish


def meet():
    row, tm = lax.axis_index("row"), lax.axis_index("tm")
    chip, core = lax.div(tm, 2), lax.rem(tm, 2)
    barrier = pltpu.get_barrier_semaphore()

    def greet_row(i, carry):
        pl.semaphore_signal(barrier, inc=1, device_id={"row": lax.rem(row + i, 8), "tm": tm})
        return carry

    def greet_chip(i, carry):
        pl.semaphore_signal(barrier, inc=1, device_id={"row": row, "tm": lax.rem(chip + i, 16) * 2 + core})
        return carry

    lax.fori_loop(1, 8, greet_row, 0)
    lax.fori_loop(1, 16, greet_chip, 0)
    pl.semaphore_signal(barrier, inc=1, device_id={"row": row, "tm": chip * 2 + 1 - core})
    pl.semaphore_wait(barrier, 23)


def cosine(freq, time):
    scale = math.sqrt((1.0 if freq == 0 else 2.0) / 32)
    return scale * math.cos(math.pi * freq * (time + 0.5) / 32)


def cosine_kernel(
    block, out, paired, times, times_more, freqs, freqs_more, gathered, gathered_more, final, final_more,
    flat, mirror, mirror_half, joined,
    swap_send, swap_recv, chip_send, chip_recv, more_send, more_recv, back_send, back_recv,
    back_more_send, back_more_recv, end_send, end_recv, mirror_send, mirror_recv,
):
    row, tm = lax.axis_index("row"), lax.axis_index("tm")
    chip, core = lax.div(tm, 2), lax.rem(tm, 2)
    partner = {"row": row, "tm": chip * 2 + 1 - core}
    has_more = lax.rem(chip, 5) == 0

    def other(i):
        return lax.rem(lax.div(chip, 4) + lax.div(i, 4), 4) * 4 + lax.rem(lax.rem(chip, 4) + lax.rem(i, 4), 4)

    def device(target):
        return {"row": row, "tm": target * 2 + core}

    def aligned(start, size):
        return pl.ds(pl.multiple_of(start, size), size)

    swap = pltpu.make_async_remote_copy(
        block.at[aligned((1 - core) * SHARE, SHARE)], paired.at[core], swap_send, swap_recv, device_id=partner,
    )
    swap.start()
    paired[core] = block[aligned(core * SHARE, SHARE)]
    swap.wait()

    def more_copy(e):
        return pltpu.make_async_remote_copy(
            paired.at[:, MAIN + e * 8:MAIN + e * 8 + 8], times_more.at[chip],
            more_send.at[e], more_recv, device_id=device(5 * e),
        )

    def spread(i, carry):
        target = other(i)
        pltpu.make_async_remote_copy(
            paired.at[:, aligned(target * 16, 16)], times.at[chip],
            chip_send, chip_recv, device_id=device(target),
        ).start()
        return carry

    lax.fori_loop(1, 16, spread, 0)
    for e in range(4):
        @pl.when(chip != 5 * e)
        def _():
            more_copy(e).start()

        @pl.when(chip == 5 * e)
        def _():
            times_more[chip] = paired[:, MAIN + e * 8:MAIN + e * 8 + 8]
    times[chip] = paired[:, aligned(chip * 16, 16)]
    pltpu.make_async_copy(times.at[pl.ds(0, 15)], times.at[pl.ds(0, 15)], chip_recv).wait()

    def transform(source, result, rows):
        at = [source[t // 2, t % 2, rows] for t in range(32)]
        mixed = ([at[t] + at[31 - t] for t in range(16)], [at[t] - at[31 - t] for t in range(16)])
        for freq in range(32):
            value = None
            for t in range(16):
                term = cosine(freq, t) * mixed[freq % 2][t]
                value = term if value is None else value + term
            result[freq // 2, freq % 2, rows] = value

    def transform_main(i, carry):
        transform(times, freqs, aligned(i * 8, 8))
        return carry

    lax.fori_loop(0, 2, transform_main, 0)

    def give(i, carry):
        target = other(i)
        pltpu.make_async_remote_copy(
            freqs.at[target], gathered.at[chip], back_send, back_recv, device_id=device(target),
        ).start()
        return carry

    lax.fori_loop(1, 16, give, 0)

    def back_more_copy(target, e):
        return pltpu.make_async_remote_copy(
            freqs_more.at[target], gathered_more.at[e],
            back_more_send, back_more_recv.at[e], device_id=device(target),
        )

    @pl.when(has_more)
    def _():
        pltpu.make_async_copy(times_more.at[pl.ds(0, 15)], times_more.at[pl.ds(0, 15)], more_recv).wait()
        transform(times_more, freqs_more, pl.ds(0, 8))

        def give_more(i, carry):
            back_more_copy(other(i), lax.div(chip, 5)).start()
            return carry

        lax.fori_loop(1, 16, give_more, 0)
        gathered_more[lax.div(chip, 5)] = freqs_more[chip]

    gathered[chip] = freqs[chip]
    pltpu.make_async_copy(gathered.at[pl.ds(0, 15)], gathered.at[pl.ds(0, 15)], back_recv).wait()
    last = pltpu.make_async_remote_copy(
        gathered.at[:, 1 - core], final.at[core], end_send.at[0], end_recv.at[0], device_id=partner
    )
    last.start()
    for e in range(4):
        @pl.when(chip != 5 * e)
        def _():
            back_more_copy(chip, e).wait_recv()
    last_more = pltpu.make_async_remote_copy(
        gathered_more.at[:, 1 - core], final_more.at[core], end_send.at[1], end_recv.at[1], device_id=partner
    )
    last_more.start()
    final[core] = gathered[:, core]
    final_more[core] = gathered_more[:, core]
    last.wait()
    last_more.wait()
    for c in range(2):
        for p in range(16):
            flat[c * SHARE + p * 16:c * SHARE + p * 16 + 16] = final[c, p]
        for e in range(4):
            flat[c * SHARE + MAIN + e * 8:c * SHARE + MAIN + e * 8 + 8] = final_more[c, e]

    mirrors = []
    place = ring_place(row)
    for d in range(1, 5):
        part, to = (pl.ds(d * TILE, TILE), mirror.at[d - 1]) if d < 4 else (pl.ds(4 * TILE, 64), mirror_half)
        mirrors.append(pltpu.make_async_remote_copy(
            flat.at[part], to, mirror_send.at[d - 1], mirror_recv.at[d - 1],
            device_id={"row": ring_row(place + d), "tm": tm},
        ))
        mirrors[-1].start()

    def columns(j):
        return aligned(ring_row(j) * TILE, TILE)

    for d in range(4):
        out[0, :, columns(place + d)] = flat[d * TILE:(d + 1) * TILE]
    for d in range(1, 4):
        mirrors[d - 1].wait_recv()
        out[0, :, columns(place + 8 - d)] = mirror[d - 1].T
    mirrors[3].wait_recv()
    upper = lax.div(place, 4)
    joined[aligned(upper * 64, 64)] = flat[4 * TILE:KEPT]
    joined[aligned((1 - upper) * 64, 64)] = mirror_half[...]

    @pl.when(upper == 0)
    def _():
        out[0, :, columns(place + 4)] = joined[...]

    @pl.when(upper == 1)
    def _():
        out[0, :, columns(place + 4)] = joined[...].T

    for copy in mirrors:
        copy.wait_send()
    pltpu.make_async_copy(times.at[pl.ds(0, 15)], times.at[pl.ds(0, 15)], chip_send).wait()
    pltpu.make_async_copy(times.at[pl.ds(0, 15)], times.at[pl.ds(0, 15)], back_send).wait()
    for e in range(4):
        @pl.when(chip != 5 * e)
        def _():
            more_copy(e).wait_send()

    @pl.when(has_more)
    def _():
        pltpu.make_async_copy(times_more.at[pl.ds(0, 15)], times_more.at[pl.ds(0, 15)], back_more_send).wait()


def kernel(occ, vir, eps, out, block, *scratch):
    meet()
    finish = green_kernel(occ, vir, eps, block, *scratch[:GREEN_SCRATCH])
    cosine_kernel(block, out, *scratch[GREEN_SCRATCH:])
    finish()


def on_device(occ_factor, vir_factor, eps_basis):
    dma = pltpu.SemaphoreType.DMA
    main = pltpu.VMEM((16, 2, 16, TILE), F32)
    more = pltpu.VMEM((16, 2, 8, TILE), F32)
    rows_sems = dma((2, 4, len(PARTS)))
    green = [
        pltpu.VMEM((2, 4 * ROWS, 2048), F32),
        pltpu.VMEM((2, 4 * ROWS, 2048), BF16),
        pltpu.VMEM((2, 4 * ROWS, 2048), BF16),
        pltpu.VMEM((4 * ROWS, 1024), F32),
        pltpu.VMEM((4 * ROWS, 1024), BF16),
        pltpu.VMEM((4 * ROWS, 1024), BF16),
        pltpu.VMEM((128, 4 * ROWS), F32),
        pltpu.VMEM((1024, 1024), F32),
        pltpu.VMEM((TILE, TILE), F32),
        pltpu.VMEM((8, KEPT, TILE), F32),
        pltpu.VMEM((8, KEPT, TILE), F32),
        dma((3,)), dma((4,)), dma((4,)), dma((4, 4)), dma((4, 4)), rows_sems, rows_sems, dma((8,)), dma((8,)),
    ]
    assert len(green) == GREEN_SCRATCH
    return pl.pallas_call(
        kernel,
        out_shape=jax.ShapeDtypeStruct((1, TILE, 1024), F32),
        in_specs=[pl.BlockSpec(memory_space=pl.ANY)] * 3,
        out_specs=pl.BlockSpec(memory_space=pltpu.VMEM),
        scratch_shapes=[
            pltpu.VMEM((KEPT, TILE), F32),
            *green,
            pltpu.VMEM((2, SHARE, TILE), F32),
            main, more, main, more, main,
            pltpu.VMEM((4, 2, 8, TILE), F32),
            pltpu.VMEM((2, 16, 16, TILE), F32),
            pltpu.VMEM((2, 4, 8, TILE), F32),
            pltpu.VMEM((KEPT, TILE), F32),
            pltpu.VMEM((3, TILE, TILE), F32),
            pltpu.VMEM((64, TILE), F32),
            pltpu.VMEM((TILE, TILE), F32),
            dma, dma, dma, dma, dma((4,)), dma, dma, dma, dma, dma((4,)), dma((2,)), dma((2,)), dma((4,)), dma((4,)),
        ],
        compiler_params=pltpu.CompilerParams(
            collective_id=0, has_side_effects=True, vmem_limit_bytes=62 << 20
        ),
        cost_estimate=pl.CostEstimate(flops=20 * 10**9, bytes_accessed=20 << 20, transcendentals=0),
        name="polarizability",
    )(occ_factor, vir_factor, eps_basis)


def solution(mesh):
    placed = (P("tm", "row", None), P("tm", "row", None), P("row", None))
    return jax.shard_map(
        on_device, mesh=mesh, in_specs=placed, out_specs=P("tm", "row", None), check_vma=False
    )
```

```python
import functools
import math

import jax
import jax.numpy as jnp
from jax import lax
from jax.experimental import pallas as pl
from jax.experimental.pallas import tpu as pltpu
from jax.sharding import PartitionSpec as P

F32 = jnp.float32
BF16 = jnp.bfloat16
NT_DIMS = (((1,), (1,)), ((), ()))
NN_DIMS = (((1,), (0,)), ((), ()))
TN_DIMS = (((0,), (0,)), ((), ()))
OWN, NEXT, ACROSS, FAR = 0, 1, 2, 3
ROWS = 256
EARLY, LATE = 192, 64
PARTS = ((0, EARLY), (EARLY, LATE))
MEETING = (EARLY, LATE + 2 * ROWS)
TILE = 128
QUARTER = 64
KEPT = 4 * TILE + 64
SHARE = KEPT // 2
MAIN = 256
GREEN_SCRATCH = 22


def ring_place(row):
    y, z = lax.div(row, 2), lax.rem(row, 2)
    return y + z * (7 - 2 * y)


def ring_row(place):
    place = lax.rem(place, 8)
    z = lax.div(place, 4)
    return (place + z * (7 - 2 * place)) * 2 + z


def halves_of(x):
    high = x.astype(BF16)
    return high, (x - high.astype(F32)).astype(BF16)


def dot3(lhs, rhs, dims):
    mul = functools.partial(lax.dot_general, dimension_numbers=dims, preferred_element_type=F32)
    return mul(lhs[0], rhs[0]) + (mul(lhs[0], rhs[1]) + mul(lhs[1], rhs[0]))


def green_kernel(
    occ, vir, eps, out, full, high, low, basis, basis_high, basis_low, polar, late, late_basis, total, turned, staged, arrived,
    local_sem, basis_send, basis_recv, share_send, share_recv, send, recv, part_send, part_recv,
):
    row, tm = lax.axis_index("row"), lax.axis_index("tm")
    y, z = lax.div(row, 2), lax.rem(row, 2)
    step = 1 - 2 * lax.rem(tm, 2)
    before = {"row": lax.rem(y - step + 4, 4) * 2 + z, "tm": tm}
    across = {"row": y * 2 + 1 - z, "tm": tm}
    x = lax.div(tm, 8)
    beside = [{"row": row, "tm": lax.rem(tm + 8 * i, 32)} for i in range(4)]

    def block(slot, chunk=None):
        if chunk is None:
            return pl.ds(slot * ROWS, ROWS)
        return pl.ds(slot * ROWS + PARTS[chunk][0], PARTS[chunk][1])

    def quarter(slot, of):
        return pl.ds(pl.multiple_of(slot * ROWS + of * QUARTER, QUARTER), QUARTER)

    def send_basis(src, slot, device):
        return pltpu.make_async_remote_copy(
            src, basis.at[quarter(slot, x)], basis_send.at[slot], basis_recv.at[slot], device_id=device
        )

    def share_basis(slot):
        copies["basis", slot].wait_recv()
        part = basis.at[quarter(slot, x)]
        for i in range(1, 4):
            copies["share", slot, i] = pltpu.make_async_remote_copy(
                part, part, share_send.at[slot, i], share_recv.at[slot, i], device_id=beside[i]
            )
            copies["share", slot, i].start()

    def take_basis(slot):
        for i in range(1, 4):
            copies["share", slot, i].wait_recv()
        convert_basis(slot)

    def send_rows(which, chunk, src, slot, device):
        return pltpu.make_async_remote_copy(
            src, full.at[which, block(slot, chunk)],
            send.at[which, slot, chunk], recv.at[which, slot, chunk], device_id=device,
        )

    sources = (occ.at[0], vir.at[0])
    copies = {}
    copies["basis", NEXT] = send_basis(eps.at[quarter(0, x)], NEXT, before)
    copies["basis", ACROSS] = send_basis(eps.at[quarter(0, x)], ACROSS, across)
    for chunk in range(len(PARTS)):
        for which in range(2):
            part = sources[which].at[pl.ds(*PARTS[chunk])]
            copies[which, NEXT, chunk] = send_rows(which, chunk, part, NEXT, before)
            copies[which, ACROSS, chunk] = send_rows(which, chunk, part, ACROSS, across)
    for copy in copies.values():
        copy.start()

    own = [pltpu.make_async_copy(sources[which], full.at[which, block(OWN)], local_sem.at[which]) for which in range(2)]
    own.append(pltpu.make_async_copy(eps, basis.at[block(OWN)], local_sem.at[2]))
    for copy in own:
        copy.start()
    for copy in own:
        copy.wait()

    def convert(slot, first, size):
        start = slot * ROWS + first

        def body(i, carry):
            rows = pl.ds(start + i * 16, 16)
            for which in range(2):
                high[which, rows], low[which, rows] = halves_of(full[which, rows])
            return carry

        lax.fori_loop(0, size // 16, body, 0)

    def convert_basis(slot):
        def body(i, carry):
            rows = pl.ds(slot * ROWS + i * 16, 16)
            basis_high[rows], basis_low[rows] = halves_of(basis[rows])
            return carry

        lax.fori_loop(0, ROWS // 16, body, 0)

    def greens(left, size, right, width, weight):
        def one(which):
            lhs = (high[which, pl.ds(left, size)], low[which, pl.ds(left, size)])
            rhs = (high[which, pl.ds(right, width)], low[which, pl.ds(right, width)])
            return dot3(lhs, rhs, NT_DIMS)

        polar[0:size, pl.ds(right, width)] = weight * (one(0) * one(1))

    def project(left, size, spans, first):
        term = None
        for start, width in spans:
            rhs = (basis_high[pl.ds(start, width)], basis_low[pl.ds(start, width)])
            new = dot3(halves_of(polar[0:size, pl.ds(start, width)]), rhs, NN_DIMS)
            term = new if term is None else term + new
        term = halves_of(term)

        def body(i, carry):
            columns = pl.ds(pl.multiple_of(i * 256, 256), 256)
            lhs = (basis_high[pl.ds(left, size), columns], basis_low[pl.ds(left, size), columns])
            new = dot3(lhs, term, TN_DIMS)
            total[columns] = new if first else total[columns] + new
            return carry

        lax.fori_loop(0, 4, body, 0)

    def convert_late(k, slot):
        def body(i, carry):
            rows = pl.ds(slot * ROWS + EARLY + i * 16, 16)
            for which in range(2):
                upper, lower = halves_of(full[which, rows])
                late[which, pl.ds(k * LATE + i * 16, 16)] = upper
                late[which, pl.ds((2 + k) * LATE + i * 16, 16)] = lower
                if slot == ACROSS:
                    high[which, rows], low[which, rows] = upper, lower
            return carry

        lax.fori_loop(0, LATE // 16, body, 0)

    def prepare_late_basis():
        for k, slot in enumerate((ACROSS, FAR)):
            rows = basis[slot * ROWS + EARLY:(slot + 1) * ROWS]
            turned[k * LATE:(k + 1) * LATE, :] = rows
        upper, lower = halves_of(turned[0:TILE].T)
        late_basis[:, 0:TILE] = upper
        late_basis[:, TILE:2 * TILE] = upper
        late_basis[:, 2 * TILE:3 * TILE] = lower

    def late_work():
        rows = pl.ds(*MEETING)

        def one(which):
            both = lax.dot_general(high[which, rows], late[which], NT_DIMS, preferred_element_type=F32)
            rest = lax.dot_general(low[which, rows], late[which, 0:TILE], NT_DIMS, preferred_element_type=F32)
            return both[:, 0:TILE] + (both[:, TILE:] + rest)

        at_row = lax.broadcasted_iota(jnp.int32, (MEETING[1], TILE), 0)
        across_side = lax.broadcasted_iota(jnp.int32, (MEETING[1], TILE), 1) < LATE
        weight = jnp.where(
            at_row < LATE, 0.5,
            jnp.where(
                at_row < LATE + ROWS, jnp.where(across_side, 1.0, 0.0),
                jnp.where(across_side, 0.0, jnp.where(at_row < LATE + ROWS + EARLY, 1.0, 0.5)),
            ),
        )
        upper, lower = halves_of((weight * (one(0) * one(1))).T)
        both = jnp.concatenate([upper, lower], axis=0)
        term = lax.dot_general(both, basis_high[rows], NN_DIMS, preferred_element_type=F32)
        term = term[0:TILE] + (
            term[TILE:] + lax.dot_general(upper, basis_low[rows], NN_DIMS, preferred_element_type=F32)
        )
        upper, lower = halves_of(term)
        rhs = jnp.concatenate([upper, lower, upper], axis=0)

        def body(i, carry):
            part = pl.ds(pl.multiple_of(i * 256, 256), 256)
            total[part] += lax.dot_general(late_basis[part], rhs, NN_DIMS, preferred_element_type=F32)
            return carry

        lax.fori_loop(0, 4, body, 0)

    def at(slot, first=0):
        return slot * ROWS + first

    def wait_rows(slot, chunk):
        for which in range(2):
            copies[which, slot, chunk].wait_recv()

    def work(slot, first, size, spans, opening=False):
        for start, width, weight in spans:
            greens(at(slot, first), size, start, width, weight)
        project(at(slot, first), size, [span[:2] for span in spans], opening)

    convert_basis(OWN)
    share_basis(NEXT)
    copies["basis", FAR] = send_basis(basis.at[quarter(NEXT, x)], FAR, before)
    copies["basis", FAR].start()
    share_basis(ACROSS)
    convert(OWN, 0, ROWS)
    work(OWN, 0, 128, [(at(OWN), ROWS, 0.5)], opening=True)
    work(OWN, 128, 128, [(at(OWN), ROWS, 0.5)])
    for chunk in range(len(PARTS)):
        wait_rows(NEXT, chunk)
        for which in range(2):
            copies[which, FAR, chunk] = send_rows(which, chunk, full.at[which, block(NEXT, chunk)], FAR, before)
            copies[which, FAR, chunk].start()
    share_basis(FAR)
    take_basis(NEXT)
    convert(NEXT, 0, ROWS)
    work(NEXT, 0, 128, [(at(OWN), ROWS, 1.0)])
    work(NEXT, 128, 128, [(at(OWN), ROWS, 1.0)])

    take_basis(ACROSS)
    take_basis(FAR)
    prepare_late_basis()
    own_weight = jnp.where(lax.broadcasted_iota(jnp.int32, (1, 2 * ROWS), 1) < EARLY, 0.5, 1.0)
    wait_rows(ACROSS, 0)
    convert(ACROSS, 0, EARLY)
    work(ACROSS, 0, EARLY, [(at(OWN), 2 * ROWS, own_weight)])
    wait_rows(FAR, 0)
    convert(FAR, 0, EARLY)
    work(FAR, 0, EARLY, [(at(OWN), ROWS, own_weight[:, 0:ROWS]), (at(ACROSS), EARLY, 0.5)])
    wait_rows(ACROSS, 1)
    convert_late(0, ACROSS)
    wait_rows(FAR, 1)
    convert_late(1, FAR)
    late_work()

    def fold(owner, slot):
        def span(j):
            return pl.ds(pl.multiple_of(j * TILE, TILE), TILE)

        rows = span(owner)
        place = ring_place(owner)
        for d in range(4):
            tile = span(ring_row(place + d))
            staged[slot, d * TILE:(d + 1) * TILE] = total[rows, tile] + total[tile, rows].T
        upper = lax.div(place, 4)
        low_tile, high_tile = ring_row(lax.rem(place, 4)), ring_row(lax.rem(place, 4) + 4)
        turned[:, 0:TILE] = total[span(high_tile), span(low_tile)].T
        half = pl.ds(pl.multiple_of(low_tile * TILE + upper * 64, 64), 64)
        staged[slot, 4 * TILE:KEPT] = (
            total[half, span(high_tile)] + turned[pl.ds(pl.multiple_of(upper * 64, 64), 64), 0:TILE]
        )

    def part_copy(owner, i):
        return pltpu.make_async_remote_copy(
            staged.at[i], arrived.at[i], part_send.at[i], part_recv.at[i],
            device_id={"row": owner, "tm": tm},
        )

    def send_part(i, carry):
        owner = lax.rem(row + i, 8)
        fold(owner, i)
        part_copy(owner, i).start()
        return carry

    lax.fori_loop(1, 8, send_part, 0)
    fold(row, 0)

    def take_part(i, carry):
        part_copy(row, i).wait_recv()
        return carry

    lax.fori_loop(1, 8, take_part, 0)

    def add(i, carry):
        rows = pl.ds(i * 64, 64)
        value = staged[0, rows]
        for j in range(1, 8):
            value = value + arrived[j, rows]
        out[rows] = value
        return carry

    lax.fori_loop(0, KEPT // 64, add, 0)

    def finish():
        for copy in copies.values():
            copy.wait_send()

        def drain(i, carry):
            part_copy(row, i).wait_send()
            return carry

        lax.fori_loop(1, 8, drain, 0)

    return finish


def meet():
    row, tm = lax.axis_index("row"), lax.axis_index("tm")
    chip, core = lax.div(tm, 2), lax.rem(tm, 2)
    barrier = pltpu.get_barrier_semaphore()

    def greet_row(i, carry):
        pl.semaphore_signal(barrier, inc=1, device_id={"row": lax.rem(row + i, 8), "tm": tm})
        return carry

    def greet_chip(i, carry):
        pl.semaphore_signal(barrier, inc=1, device_id={"row": row, "tm": lax.rem(chip + i, 16) * 2 + core})
        return carry

    lax.fori_loop(1, 8, greet_row, 0)
    lax.fori_loop(1, 16, greet_chip, 0)
    pl.semaphore_signal(barrier, inc=1, device_id={"row": row, "tm": chip * 2 + 1 - core})
    pl.semaphore_wait(barrier, 23)


def cosine(freq, time):
    scale = math.sqrt((1.0 if freq == 0 else 2.0) / 32)
    return scale * math.cos(math.pi * freq * (time + 0.5) / 32)


def cosine_kernel(
    block, out, paired, times, times_more, freqs, freqs_more, gathered, gathered_more, final, final_more,
    flat, mirror, mirror_half, joined,
    swap_send, swap_recv, chip_send, chip_recv, more_send, more_recv, back_send, back_recv,
    back_more_send, back_more_recv, end_send, end_recv, mirror_send, mirror_recv,
):
    row, tm = lax.axis_index("row"), lax.axis_index("tm")
    chip, core = lax.div(tm, 2), lax.rem(tm, 2)
    partner = {"row": row, "tm": chip * 2 + 1 - core}
    has_more = lax.rem(chip, 5) == 0

    def other(i):
        return lax.rem(lax.div(chip, 4) + lax.div(i, 4), 4) * 4 + lax.rem(lax.rem(chip, 4) + lax.rem(i, 4), 4)

    def device(target):
        return {"row": row, "tm": target * 2 + core}

    def aligned(start, size):
        return pl.ds(pl.multiple_of(start, size), size)

    swap = pltpu.make_async_remote_copy(
        block.at[aligned((1 - core) * SHARE, SHARE)], paired.at[core], swap_send, swap_recv, device_id=partner,
    )
    swap.start()
    paired[core] = block[aligned(core * SHARE, SHARE)]
    swap.wait()

    def more_copy(e):
        return pltpu.make_async_remote_copy(
            paired.at[:, MAIN + e * 8:MAIN + e * 8 + 8], times_more.at[chip],
            more_send.at[e], more_recv, device_id=device(5 * e),
        )

    def spread(i, carry):
        target = other(i)
        pltpu.make_async_remote_copy(
            paired.at[:, aligned(target * 16, 16)], times.at[chip],
            chip_send, chip_recv, device_id=device(target),
        ).start()
        return carry

    lax.fori_loop(1, 16, spread, 0)
    for e in range(4):
        @pl.when(chip != 5 * e)
        def _():
            more_copy(e).start()

        @pl.when(chip == 5 * e)
        def _():
            times_more[chip] = paired[:, MAIN + e * 8:MAIN + e * 8 + 8]
    times[chip] = paired[:, aligned(chip * 16, 16)]
    pltpu.make_async_copy(times.at[pl.ds(0, 15)], times.at[pl.ds(0, 15)], chip_recv).wait()

    def transform(source, result, rows):
        at = [source[t // 2, t % 2, rows] for t in range(32)]
        mixed = ([at[t] + at[31 - t] for t in range(16)], [at[t] - at[31 - t] for t in range(16)])
        for freq in range(32):
            value = None
            for t in range(16):
                term = cosine(freq, t) * mixed[freq % 2][t]
                value = term if value is None else value + term
            result[freq // 2, freq % 2, rows] = value

    def transform_main(i, carry):
        transform(times, freqs, aligned(i * 8, 8))
        return carry

    lax.fori_loop(0, 2, transform_main, 0)

    def give(i, carry):
        target = other(i)
        pltpu.make_async_remote_copy(
            freqs.at[target], gathered.at[chip], back_send, back_recv, device_id=device(target),
        ).start()
        return carry

    lax.fori_loop(1, 16, give, 0)

    def back_more_copy(target, e):
        return pltpu.make_async_remote_copy(
            freqs_more.at[target], gathered_more.at[e],
            back_more_send, back_more_recv.at[e], device_id=device(target),
        )

    @pl.when(has_more)
    def _():
        pltpu.make_async_copy(times_more.at[pl.ds(0, 15)], times_more.at[pl.ds(0, 15)], more_recv).wait()
        transform(times_more, freqs_more, pl.ds(0, 8))

        def give_more(i, carry):
            back_more_copy(other(i), lax.div(chip, 5)).start()
            return carry

        lax.fori_loop(1, 16, give_more, 0)
        gathered_more[lax.div(chip, 5)] = freqs_more[chip]

    gathered[chip] = freqs[chip]
    pltpu.make_async_copy(gathered.at[pl.ds(0, 15)], gathered.at[pl.ds(0, 15)], back_recv).wait()
    last = pltpu.make_async_remote_copy(
        gathered.at[:, 1 - core], final.at[core], end_send.at[0], end_recv.at[0], device_id=partner
    )
    last.start()
    for e in range(4):
        @pl.when(chip != 5 * e)
        def _():
            back_more_copy(chip, e).wait_recv()
    last_more = pltpu.make_async_remote_copy(
        gathered_more.at[:, 1 - core], final_more.at[core], end_send.at[1], end_recv.at[1], device_id=partner
    )
    last_more.start()
    final[core] = gathered[:, core]
    final_more[core] = gathered_more[:, core]
    last.wait()
    last_more.wait()
    for c in range(2):
        for p in range(16):
            flat[c * SHARE + p * 16:c * SHARE + p * 16 + 16] = final[c, p]
        for e in range(4):
            flat[c * SHARE + MAIN + e * 8:c * SHARE + MAIN + e * 8 + 8] = final_more[c, e]

    mirrors = []
    place = ring_place(row)
    for d in range(1, 5):
        part, to = (pl.ds(d * TILE, TILE), mirror.at[d - 1]) if d < 4 else (pl.ds(4 * TILE, 64), mirror_half)
        mirrors.append(pltpu.make_async_remote_copy(
            flat.at[part], to, mirror_send.at[d - 1], mirror_recv.at[d - 1],
            device_id={"row": ring_row(place + d), "tm": tm},
        ))
        mirrors[-1].start()

    def columns(j):
        return aligned(ring_row(j) * TILE, TILE)

    for d in range(4):
        out[0, :, columns(place + d)] = flat[d * TILE:(d + 1) * TILE]
    for d in range(1, 4):
        mirrors[d - 1].wait_recv()
        out[0, :, columns(place + 8 - d)] = mirror[d - 1].T
    mirrors[3].wait_recv()
    upper = lax.div(place, 4)
    joined[aligned(upper * 64, 64)] = flat[4 * TILE:KEPT]
    joined[aligned((1 - upper) * 64, 64)] = mirror_half[...]

    @pl.when(upper == 0)
    def _():
        out[0, :, columns(place + 4)] = joined[...]

    @pl.when(upper == 1)
    def _():
        out[0, :, columns(place + 4)] = joined[...].T

    for copy in mirrors:
        copy.wait_send()
    pltpu.make_async_copy(times.at[pl.ds(0, 15)], times.at[pl.ds(0, 15)], chip_send).wait()
    pltpu.make_async_copy(times.at[pl.ds(0, 15)], times.at[pl.ds(0, 15)], back_send).wait()
    for e in range(4):
        @pl.when(chip != 5 * e)
        def _():
            more_copy(e).wait_send()

    @pl.when(has_more)
    def _():
        pltpu.make_async_copy(times_more.at[pl.ds(0, 15)], times_more.at[pl.ds(0, 15)], back_more_send).wait()


def kernel(occ, vir, eps, out, block, *scratch):
    meet()
    finish = green_kernel(occ, vir, eps, block, *scratch[:GREEN_SCRATCH])
    cosine_kernel(block, out, *scratch[GREEN_SCRATCH:])
    finish()


def on_device(occ_factor, vir_factor, eps_basis):
    dma = pltpu.SemaphoreType.DMA
    main = pltpu.VMEM((16, 2, 16, TILE), F32)
    more = pltpu.VMEM((16, 2, 8, TILE), F32)
    rows_sems = dma((2, 4, len(PARTS)))
    green = [
        pltpu.VMEM((2, 4 * ROWS, 2048), F32),
        pltpu.VMEM((2, 4 * ROWS, 2048), BF16),
        pltpu.VMEM((2, 4 * ROWS, 2048), BF16),
        pltpu.VMEM((4 * ROWS, 1024), F32),
        pltpu.VMEM((4 * ROWS, 1024), BF16),
        pltpu.VMEM((4 * ROWS, 1024), BF16),
        pltpu.VMEM((EARLY, 4 * ROWS), F32),
        pltpu.VMEM((2, 4 * LATE, 2048), BF16),
        pltpu.VMEM((1024, 3 * TILE), BF16),
        pltpu.VMEM((1024, 1024), F32),
        pltpu.VMEM((TILE, 1024), F32),
        pltpu.VMEM((8, KEPT, TILE), F32),
        pltpu.VMEM((8, KEPT, TILE), F32),
        dma((3,)), dma((4,)), dma((4,)), dma((4, 4)), dma((4, 4)), rows_sems, rows_sems, dma((8,)), dma((8,)),
    ]
    assert len(green) == GREEN_SCRATCH
    return pl.pallas_call(
        kernel,
        out_shape=jax.ShapeDtypeStruct((1, TILE, 1024), F32),
        in_specs=[pl.BlockSpec(memory_space=pl.ANY)] * 3,
        out_specs=pl.BlockSpec(memory_space=pltpu.VMEM),
        scratch_shapes=[
            pltpu.VMEM((KEPT, TILE), F32),
            *green,
            pltpu.VMEM((2, SHARE, TILE), F32),
            main, more, main, more, main,
            pltpu.VMEM((4, 2, 8, TILE), F32),
            pltpu.VMEM((2, 16, 16, TILE), F32),
            pltpu.VMEM((2, 4, 8, TILE), F32),
            pltpu.VMEM((KEPT, TILE), F32),
            pltpu.VMEM((3, TILE, TILE), F32),
            pltpu.VMEM((64, TILE), F32),
            pltpu.VMEM((TILE, TILE), F32),
            dma, dma, dma, dma, dma((4,)), dma, dma, dma, dma, dma((4,)), dma((2,)), dma((2,)), dma((4,)), dma((4,)),
        ],
        compiler_params=pltpu.CompilerParams(
            collective_id=0, has_side_effects=True, vmem_limit_bytes=62 << 20
        ),
        cost_estimate=pl.CostEstimate(flops=20 * 10**9, bytes_accessed=20 << 20, transcendentals=0),
        name="polarizability",
    )(occ_factor, vir_factor, eps_basis)


def solution(mesh):
    placed = (P("tm", "row", None), P("tm", "row", None), P("row", None))
    return jax.shard_map(
        on_device, mesh=mesh, in_specs=placed, out_specs=P("tm", "row", None), check_vma=False
    )
```

```python
import functools
import math

import jax
import jax.numpy as jnp
from jax import lax
from jax.experimental import pallas as pl
from jax.experimental.pallas import tpu as pltpu
from jax.sharding import PartitionSpec as P

F32 = jnp.float32
BF16 = jnp.bfloat16
NT_DIMS = (((1,), (1,)), ((), ()))
NN_DIMS = (((1,), (0,)), ((), ()))
TN_DIMS = (((0,), (0,)), ((), ()))
OWN, NEXT, ACROSS, FAR = 0, 1, 2, 3
ROWS = 256
EARLY, LATE = 192, 64
PARTS = ((0, EARLY), (EARLY, LATE))
MEETING = (EARLY, LATE + 2 * ROWS)
TILE = 128
QUARTER = 64
KEPT = 4 * TILE + 64
SHARE = KEPT // 2
MAIN = 256
GREEN_SCRATCH = 22


def ring_place(row):
    y, z = lax.div(row, 2), lax.rem(row, 2)
    return y + z * (7 - 2 * y)


def ring_row(place):
    place = lax.rem(place, 8)
    z = lax.div(place, 4)
    return (place + z * (7 - 2 * place)) * 2 + z


def halves_of(x):
    high = x.astype(BF16)
    return high, (x - high.astype(F32)).astype(BF16)


def dot3(lhs, rhs, dims):
    mul = functools.partial(lax.dot_general, dimension_numbers=dims, preferred_element_type=F32)
    return mul(lhs[0], rhs[0]) + (mul(lhs[0], rhs[1]) + mul(lhs[1], rhs[0]))


def green_kernel(
    occ, vir, eps, full, high, low, basis, basis_high, basis_low, polar, late, late_basis, total, turned, staged, arrived,
    local_sem, basis_send, basis_recv, share_send, share_recv, send, recv, part_send, part_recv,
):
    row, tm = lax.axis_index("row"), lax.axis_index("tm")
    y, z = lax.div(row, 2), lax.rem(row, 2)
    step = 1 - 2 * lax.rem(tm, 2)
    before = {"row": lax.rem(y - step + 4, 4) * 2 + z, "tm": tm}
    across = {"row": y * 2 + 1 - z, "tm": tm}
    x = lax.div(tm, 8)
    beside = [{"row": row, "tm": lax.rem(tm + 8 * i, 32)} for i in range(4)]

    def block(slot, chunk=None):
        if chunk is None:
            return pl.ds(slot * ROWS, ROWS)
        return pl.ds(slot * ROWS + PARTS[chunk][0], PARTS[chunk][1])

    def quarter(slot, of):
        return pl.ds(pl.multiple_of(slot * ROWS + of * QUARTER, QUARTER), QUARTER)

    def send_basis(src, slot, device):
        return pltpu.make_async_remote_copy(
            src, basis.at[quarter(slot, x)], basis_send.at[slot], basis_recv.at[slot], device_id=device
        )

    def share_basis(slot):
        copies["basis", slot].wait_recv()
        part = basis.at[quarter(slot, x)]
        for i in range(1, 4):
            copies["share", slot, i] = pltpu.make_async_remote_copy(
                part, part, share_send.at[slot, i], share_recv.at[slot, i], device_id=beside[i]
            )
            copies["share", slot, i].start()

    def take_basis(slot):
        for i in range(1, 4):
            copies["share", slot, i].wait_recv()
        convert_basis(slot)

    def send_rows(which, chunk, src, slot, device):
        return pltpu.make_async_remote_copy(
            src, full.at[which, block(slot, chunk)],
            send.at[which, slot, chunk], recv.at[which, slot, chunk], device_id=device,
        )

    sources = (occ.at[0], vir.at[0])
    copies = {}
    copies["basis", NEXT] = send_basis(eps.at[quarter(0, x)], NEXT, before)
    copies["basis", ACROSS] = send_basis(eps.at[quarter(0, x)], ACROSS, across)
    for chunk in range(len(PARTS)):
        for which in range(2):
            part = sources[which].at[pl.ds(*PARTS[chunk])]
            copies[which, NEXT, chunk] = send_rows(which, chunk, part, NEXT, before)
            copies[which, ACROSS, chunk] = send_rows(which, chunk, part, ACROSS, across)
    for copy in copies.values():
        copy.start()

    own = [pltpu.make_async_copy(sources[which], full.at[which, block(OWN)], local_sem.at[which]) for which in range(2)]
    own.append(pltpu.make_async_copy(eps, basis.at[block(OWN)], local_sem.at[2]))
    for copy in own:
        copy.start()
    for copy in own:
        copy.wait()

    def convert(slot, first, size):
        start = slot * ROWS + first

        def body(i, carry):
            rows = pl.ds(start + i * 16, 16)
            for which in range(2):
                high[which, rows], low[which, rows] = halves_of(full[which, rows])
            return carry

        lax.fori_loop(0, size // 16, body, 0)

    def convert_basis(slot):
        def body(i, carry):
            rows = pl.ds(slot * ROWS + i * 16, 16)
            basis_high[rows], basis_low[rows] = halves_of(basis[rows])
            return carry

        lax.fori_loop(0, ROWS // 16, body, 0)

    def greens(left, size, right, width, weight):
        def one(which):
            lhs = (high[which, pl.ds(left, size)], low[which, pl.ds(left, size)])
            rhs = (high[which, pl.ds(right, width)], low[which, pl.ds(right, width)])
            return dot3(lhs, rhs, NT_DIMS)

        polar[0:size, pl.ds(right, width)] = weight * (one(0) * one(1))

    def project(left, size, spans, first):
        term = None
        for start, width in spans:
            rhs = (basis_high[pl.ds(start, width)], basis_low[pl.ds(start, width)])
            new = dot3(halves_of(polar[0:size, pl.ds(start, width)]), rhs, NN_DIMS)
            term = new if term is None else term + new
        term = halves_of(term)

        def body(i, carry):
            columns = pl.ds(pl.multiple_of(i * 256, 256), 256)
            lhs = (basis_high[pl.ds(left, size), columns], basis_low[pl.ds(left, size), columns])
            new = dot3(lhs, term, TN_DIMS)
            total[columns] = new if first else total[columns] + new
            return carry

        lax.fori_loop(0, 4, body, 0)

    def convert_late(k, slot):
        def body(i, carry):
            rows = pl.ds(slot * ROWS + EARLY + i * 16, 16)
            for which in range(2):
                upper, lower = halves_of(full[which, rows])
                late[which, pl.ds(k * LATE + i * 16, 16)] = upper
                late[which, pl.ds((2 + k) * LATE + i * 16, 16)] = lower
                if slot == ACROSS:
                    high[which, rows], low[which, rows] = upper, lower
            return carry

        lax.fori_loop(0, LATE // 16, body, 0)

    def prepare_late_basis():
        for k, slot in enumerate((ACROSS, FAR)):
            rows = basis[slot * ROWS + EARLY:(slot + 1) * ROWS]
            turned[k * LATE:(k + 1) * LATE, :] = rows
        upper, lower = halves_of(turned[0:TILE].T)
        late_basis[:, 0:TILE] = upper
        late_basis[:, TILE:2 * TILE] = upper
        late_basis[:, 2 * TILE:3 * TILE] = lower

    def late_work():
        rows = pl.ds(*MEETING)

        def one(which):
            both = lax.dot_general(high[which, rows], late[which], NT_DIMS, preferred_element_type=F32)
            rest = lax.dot_general(low[which, rows], late[which, 0:TILE], NT_DIMS, preferred_element_type=F32)
            return both[:, 0:TILE] + (both[:, TILE:] + rest)

        at_row = lax.broadcasted_iota(jnp.int32, (MEETING[1], TILE), 0)
        across_side = lax.broadcasted_iota(jnp.int32, (MEETING[1], TILE), 1) < LATE
        weight = jnp.where(
            at_row < LATE, 0.5,
            jnp.where(
                at_row < LATE + ROWS, jnp.where(across_side, 1.0, 0.0),
                jnp.where(across_side, 0.0, jnp.where(at_row < LATE + ROWS + EARLY, 1.0, 0.5)),
            ),
        )
        upper, lower = halves_of((weight * (one(0) * one(1))).T)
        both = jnp.concatenate([upper, lower], axis=0)
        term = lax.dot_general(both, basis_high[rows], NN_DIMS, preferred_element_type=F32)
        term = term[0:TILE] + (
            term[TILE:] + lax.dot_general(upper, basis_low[rows], NN_DIMS, preferred_element_type=F32)
        )
        upper, lower = halves_of(term)
        rhs = jnp.concatenate([upper, lower, upper], axis=0)

        def body(i, carry):
            part = pl.ds(pl.multiple_of(i * 256, 256), 256)
            total[part] += lax.dot_general(late_basis[part], rhs, NN_DIMS, preferred_element_type=F32)
            return carry

        lax.fori_loop(0, 4, body, 0)

    def at(slot, first=0):
        return slot * ROWS + first

    def wait_rows(slot, chunk):
        for which in range(2):
            copies[which, slot, chunk].wait_recv()

    def work(slot, first, size, spans, opening=False):
        for start, width, weight in spans:
            greens(at(slot, first), size, start, width, weight)
        project(at(slot, first), size, [span[:2] for span in spans], opening)

    convert_basis(OWN)
    share_basis(NEXT)
    copies["basis", FAR] = send_basis(basis.at[quarter(NEXT, x)], FAR, before)
    copies["basis", FAR].start()
    share_basis(ACROSS)
    convert(OWN, 0, ROWS)
    work(OWN, 0, 128, [(at(OWN), ROWS, 0.5)], opening=True)
    work(OWN, 128, 128, [(at(OWN), ROWS, 0.5)])
    for chunk in range(len(PARTS)):
        wait_rows(NEXT, chunk)
        for which in range(2):
            copies[which, FAR, chunk] = send_rows(which, chunk, full.at[which, block(NEXT, chunk)], FAR, before)
            copies[which, FAR, chunk].start()
    share_basis(FAR)
    take_basis(NEXT)
    convert(NEXT, 0, ROWS)
    work(NEXT, 0, 128, [(at(OWN), ROWS, 1.0)])
    work(NEXT, 128, 128, [(at(OWN), ROWS, 1.0)])

    take_basis(ACROSS)
    take_basis(FAR)
    prepare_late_basis()
    own_weight = jnp.where(lax.broadcasted_iota(jnp.int32, (1, 2 * ROWS), 1) < EARLY, 0.5, 1.0)
    wait_rows(ACROSS, 0)
    convert(ACROSS, 0, EARLY)
    work(ACROSS, 0, EARLY, [(at(OWN), 2 * ROWS, own_weight)])
    wait_rows(FAR, 0)
    convert(FAR, 0, EARLY)
    work(FAR, 0, EARLY, [(at(OWN), ROWS, own_weight[:, 0:ROWS]), (at(ACROSS), EARLY, 0.5)])
    wait_rows(ACROSS, 1)
    convert_late(0, ACROSS)
    wait_rows(FAR, 1)
    convert_late(1, FAR)
    late_work()

    def fold(owner, slot):
        def span(j):
            return pl.ds(pl.multiple_of(j * TILE, TILE), TILE)

        rows = span(owner)
        place = ring_place(owner)
        for d in range(4):
            tile = span(ring_row(place + d))
            staged[slot, d * TILE:(d + 1) * TILE] = total[rows, tile] + total[tile, rows].T
        upper = lax.div(place, 4)
        low_tile, high_tile = ring_row(lax.rem(place, 4)), ring_row(lax.rem(place, 4) + 4)
        turned[:, 0:TILE] = total[span(high_tile), span(low_tile)].T
        half = pl.ds(pl.multiple_of(low_tile * TILE + upper * 64, 64), 64)
        staged[slot, 4 * TILE:KEPT] = (
            total[half, span(high_tile)] + turned[pl.ds(pl.multiple_of(upper * 64, 64), 64), 0:TILE]
        )

    core = lax.rem(tm, 2)

    def half_rows(half):
        return pl.ds(pl.multiple_of(half * SHARE, SHARE), SHARE)

    def part_copy(owner, i, half):
        return pltpu.make_async_remote_copy(
            staged.at[i, half_rows(half)], arrived.at[i, half_rows(half)], part_send.at[half, i], part_recv.at[half, i],
            device_id={"row": owner, "tm": tm},
        )

    def send_first(i, carry):
        owner = lax.rem(row + i, 8)
        fold(owner, i)
        part_copy(owner, i, 1 - core).start()
        return carry

    def send_second(i, carry):
        part_copy(lax.rem(row + i, 8), i, core).start()
        return carry

    lax.fori_loop(1, 8, send_first, 0)
    lax.fori_loop(1, 8, send_second, 0)
    fold(row, 0)

    def reduce_half(half, result):
        def take_part(i, carry):
            part_copy(row, i, half).wait_recv()
            return carry

        lax.fori_loop(1, 8, take_part, 0)

        def add(i, carry):
            rows = pl.ds(pl.multiple_of(half * SHARE + i * 32, 32), 32)
            value = staged[0, rows]
            for j in range(1, 8):
                value = value + arrived[j, rows]
            result[pl.ds(pl.multiple_of(i * 32, 32), 32)] = value
            return carry

        lax.fori_loop(0, SHARE // 32, add, 0)

    def finish():
        for copy in copies.values():
            copy.wait_send()

        def drain(i, carry):
            for half in range(2):
                part_copy(row, i, half).wait_send()
            return carry

        lax.fori_loop(1, 8, drain, 0)

    return reduce_half, finish


def meet():
    row, tm = lax.axis_index("row"), lax.axis_index("tm")
    chip, core = lax.div(tm, 2), lax.rem(tm, 2)
    barrier = pltpu.get_barrier_semaphore()

    def greet_row(i, carry):
        pl.semaphore_signal(barrier, inc=1, device_id={"row": lax.rem(row + i, 8), "tm": tm})
        return carry

    def greet_chip(i, carry):
        pl.semaphore_signal(barrier, inc=1, device_id={"row": row, "tm": lax.rem(chip + i, 16) * 2 + core})
        return carry

    lax.fori_loop(1, 8, greet_row, 0)
    lax.fori_loop(1, 16, greet_chip, 0)
    pl.semaphore_signal(barrier, inc=1, device_id={"row": row, "tm": chip * 2 + 1 - core})
    pl.semaphore_wait(barrier, 23)


def cosine(freq, time):
    scale = math.sqrt((1.0 if freq == 0 else 2.0) / 32)
    return scale * math.cos(math.pi * freq * (time + 0.5) / 32)


def cosine_kernel(
    reduce_half, out, for_partner, paired, times, times_more, freqs, freqs_more, gathered, gathered_more,
    final, final_more, flat, mirror, mirror_half, joined,
    swap_send, swap_recv, chip_send, chip_recv, more_send, more_recv, back_send, back_recv,
    back_more_send, back_more_recv, end_send, end_recv, mirror_send, mirror_recv,
):
    row, tm = lax.axis_index("row"), lax.axis_index("tm")
    chip, core = lax.div(tm, 2), lax.rem(tm, 2)
    partner = {"row": row, "tm": chip * 2 + 1 - core}
    has_more = lax.rem(chip, 5) == 0

    def other(i):
        return lax.rem(lax.div(chip, 4) + lax.div(i, 4), 4) * 4 + lax.rem(lax.rem(chip, 4) + lax.rem(i, 4), 4)

    def device(target):
        return {"row": row, "tm": target * 2 + core}

    def aligned(start, size):
        return pl.ds(pl.multiple_of(start, size), size)

    def wait_bytes(ref, sem):
        pltpu.make_async_copy(ref, ref, sem).wait()

    swap = pltpu.make_async_remote_copy(for_partner, paired.at[core], swap_send, swap_recv, device_id=partner)
    reduce_half(1 - core, for_partner)
    swap.start()

    def more_copy(which, e):
        return pltpu.make_async_remote_copy(
            paired.at[which, MAIN + e * 8:MAIN + e * 8 + 8], times_more.at[which, chip],
            more_send.at[which, e], more_recv.at[which], device_id=device(5 * e),
        )

    def spread(which):
        def one(i, carry):
            target = other(i)
            pltpu.make_async_remote_copy(
                paired.at[which, aligned(target * 16, 16)], times.at[which, chip],
                chip_send.at[which], chip_recv.at[which], device_id=device(target),
            ).start()
            return carry

        lax.fori_loop(1, 16, one, 0)
        for e in range(4):
            @pl.when(chip != 5 * e)
            def _():
                more_copy(which, e).start()

            @pl.when(chip == 5 * e)
            def _():
                times_more[which, chip] = paired[which, MAIN + e * 8:MAIN + e * 8 + 8]
        times[which, chip] = paired[which, aligned(chip * 16, 16)]

    swap.wait_recv()
    spread(1 - core)
    reduce_half(core, paired.at[core])
    spread(core)
    for which in range(2):
        wait_bytes(times.at[which, pl.ds(0, 15)], chip_recv.at[which])

    @pl.when(has_more)
    def _():
        for which in range(2):
            wait_bytes(times_more.at[which, pl.ds(0, 15)], more_recv.at[which])

    def transform(source, result, rows, parity):
        at = [source[t % 2, t // 2, rows] for t in range(32)]
        if parity:
            mixed = [at[t] - at[31 - t] for t in range(16)]
        else:
            mixed = [at[t] + at[31 - t] for t in range(16)]
        for freq in range(parity, 32, 2):
            value = None
            for t in range(16):
                term = cosine(freq, t) * mixed[t]
                value = term if value is None else value + term
            result[parity, freq // 2, rows] = value

    def transform_all(which):
        for parity in range(2):
            @pl.when(which == parity)
            def _():
                def main(i, carry):
                    transform(times, freqs, aligned(i * 8, 8), parity)
                    return carry

                lax.fori_loop(0, 2, main, 0)

                @pl.when(has_more)
                def _():
                    transform(times_more, freqs_more, pl.ds(0, 8), parity)

    def back_more_copy(which, target, e):
        return pltpu.make_async_remote_copy(
            freqs_more.at[which, target], gathered_more.at[which, e],
            back_more_send.at[which], back_more_recv.at[which, e], device_id=device(target),
        )

    def give(which):
        def one(i, carry):
            target = other(i)
            pltpu.make_async_remote_copy(
                freqs.at[which, target], gathered.at[which, chip],
                back_send.at[which], back_recv.at[which], device_id=device(target),
            ).start()
            return carry

        lax.fori_loop(1, 16, one, 0)

        @pl.when(has_more)
        def _():
            def one_more(i, carry):
                back_more_copy(which, other(i), lax.div(chip, 5)).start()
                return carry

            lax.fori_loop(1, 16, one_more, 0)
            gathered_more[which, lax.div(chip, 5)] = freqs_more[which, chip]

        gathered[which, chip] = freqs[which, chip]

    def take(which):
        wait_bytes(gathered.at[which, pl.ds(0, 15)], back_recv.at[which])
        for e in range(4):
            @pl.when(chip != 5 * e)
            def _():
                back_more_copy(which, chip, e).wait_recv()

    for which in (1 - core, core):
        transform_all(which)
        give(which)
    take(1 - core)
    last = pltpu.make_async_remote_copy(
        gathered.at[1 - core], final.at[core], end_send.at[0], end_recv.at[0], device_id=partner
    )
    last_more = pltpu.make_async_remote_copy(
        gathered_more.at[1 - core], final_more.at[core], end_send.at[1], end_recv.at[1], device_id=partner
    )
    last.start()
    last_more.start()
    take(core)
    final[core] = gathered[core]
    final_more[core] = gathered_more[core]
    last.wait_recv()
    last_more.wait_recv()
    for c in range(2):
        for p in range(16):
            flat[c * SHARE + p * 16:c * SHARE + p * 16 + 16] = final[c, p]
        for e in range(4):
            flat[c * SHARE + MAIN + e * 8:c * SHARE + MAIN + e * 8 + 8] = final_more[c, e]

    mirrors = []
    place = ring_place(row)
    for d in range(1, 5):
        part, to = (pl.ds(d * TILE, TILE), mirror.at[d - 1]) if d < 4 else (pl.ds(4 * TILE, 64), mirror_half)
        mirrors.append(pltpu.make_async_remote_copy(
            flat.at[part], to, mirror_send.at[d - 1], mirror_recv.at[d - 1],
            device_id={"row": ring_row(place + d), "tm": tm},
        ))
        mirrors[-1].start()

    def columns(j):
        return aligned(ring_row(j) * TILE, TILE)

    for d in range(4):
        out[0, :, columns(place + d)] = flat[d * TILE:(d + 1) * TILE]
    for d in range(1, 4):
        mirrors[d - 1].wait_recv()
        out[0, :, columns(place + 8 - d)] = mirror[d - 1].T
    mirrors[3].wait_recv()
    upper = lax.div(place, 4)
    joined[aligned(upper * 64, 64)] = flat[4 * TILE:KEPT]
    joined[aligned((1 - upper) * 64, 64)] = mirror_half[...]

    @pl.when(upper == 0)
    def _():
        out[0, :, columns(place + 4)] = joined[...]

    @pl.when(upper == 1)
    def _():
        out[0, :, columns(place + 4)] = joined[...].T

    for copy in [*mirrors, swap, last, last_more]:
        copy.wait_send()
    for which in range(2):
        wait_bytes(times.at[which, pl.ds(0, 15)], chip_send.at[which])
        wait_bytes(times.at[which, pl.ds(0, 15)], back_send.at[which])
        for e in range(4):
            @pl.when(chip != 5 * e)
            def _():
                more_copy(which, e).wait_send()

    @pl.when(has_more)
    def _():
        for which in range(2):
            wait_bytes(times_more.at[which, pl.ds(0, 15)], back_more_send.at[which])


def kernel(occ, vir, eps, out, *scratch):
    meet()
    reduce_half, finish = green_kernel(occ, vir, eps, *scratch[:GREEN_SCRATCH])
    cosine_kernel(reduce_half, out, *scratch[GREEN_SCRATCH:])
    finish()


def on_device(occ_factor, vir_factor, eps_basis):
    dma = pltpu.SemaphoreType.DMA
    main = pltpu.VMEM((2, 16, 16, TILE), F32)
    more = pltpu.VMEM((2, 16, 8, TILE), F32)
    rows_sems = dma((2, 4, len(PARTS)))
    green = [
        pltpu.VMEM((2, 4 * ROWS, 2048), F32),
        pltpu.VMEM((2, 4 * ROWS, 2048), BF16),
        pltpu.VMEM((2, 4 * ROWS, 2048), BF16),
        pltpu.VMEM((4 * ROWS, 1024), F32),
        pltpu.VMEM((4 * ROWS, 1024), BF16),
        pltpu.VMEM((4 * ROWS, 1024), BF16),
        pltpu.VMEM((EARLY, 4 * ROWS), F32),
        pltpu.VMEM((2, 4 * LATE, 2048), BF16),
        pltpu.VMEM((1024, 3 * TILE), BF16),
        pltpu.VMEM((1024, 1024), F32),
        pltpu.VMEM((TILE, 1024), F32),
        pltpu.VMEM((8, KEPT, TILE), F32),
        pltpu.VMEM((8, KEPT, TILE), F32),
        dma((3,)), dma((4,)), dma((4,)), dma((4, 4)), dma((4, 4)), rows_sems, rows_sems, dma((2, 8)), dma((2, 8)),
    ]
    assert len(green) == GREEN_SCRATCH
    return pl.pallas_call(
        kernel,
        out_shape=jax.ShapeDtypeStruct((1, TILE, 1024), F32),
        in_specs=[pl.BlockSpec(memory_space=pl.ANY)] * 3,
        out_specs=pl.BlockSpec(memory_space=pltpu.VMEM),
        scratch_shapes=[
            *green,
            pltpu.VMEM((SHARE, TILE), F32),
            pltpu.VMEM((2, SHARE, TILE), F32),
            main, more, main, more, main,
            pltpu.VMEM((2, 4, 8, TILE), F32),
            main,
            pltpu.VMEM((2, 4, 8, TILE), F32),
            pltpu.VMEM((KEPT, TILE), F32),
            pltpu.VMEM((3, TILE, TILE), F32),
            pltpu.VMEM((64, TILE), F32),
            pltpu.VMEM((TILE, TILE), F32),
            dma, dma, dma((2,)), dma((2,)), dma((2, 4)), dma((2,)), dma((2,)), dma((2,)), dma((2,)), dma((2, 4)), dma((2,)), dma((2,)),
            dma((4,)), dma((4,)),
        ],
        compiler_params=pltpu.CompilerParams(
            collective_id=0, has_side_effects=True, vmem_limit_bytes=62 << 20
        ),
        cost_estimate=pl.CostEstimate(flops=20 * 10**9, bytes_accessed=20 << 20, transcendentals=0),
        name="polarizability",
    )(occ_factor, vir_factor, eps_basis)


def solution(mesh):
    placed = (P("tm", "row", None), P("tm", "row", None), P("row", None))
    return jax.shard_map(
        on_device, mesh=mesh, in_specs=placed, out_specs=P("tm", "row", None), check_vma=False
    )
```

```python
import functools
import math

import jax
import jax.numpy as jnp
from jax import lax
from jax.experimental import pallas as pl
from jax.experimental.pallas import tpu as pltpu
from jax.sharding import PartitionSpec as P

F32 = jnp.float32
BF16 = jnp.bfloat16
NT_DIMS = (((1,), (1,)), ((), ()))
NN_DIMS = (((1,), (0,)), ((), ()))
TN_DIMS = (((0,), (0,)), ((), ()))
OWN, NEXT, ACROSS, FAR = 0, 1, 2, 3
ROWS = 256
EARLY, LATE = 192, 64
PARTS = ((0, EARLY), (EARLY, LATE))
MEETING = (EARLY, LATE + 2 * ROWS)
TILE = 128
QUARTER = 64
KEPT = 4 * TILE + 64
SHARE = KEPT // 2
MAIN = 256
GREEN_SCRATCH = 24


def ring_place(row):
    y, z = lax.div(row, 2), lax.rem(row, 2)
    return y + z * (7 - 2 * y)


def ring_row(place):
    place = lax.rem(place, 8)
    z = lax.div(place, 4)
    return (place + z * (7 - 2 * place)) * 2 + z


def halves_of(x):
    high = x.astype(BF16)
    return high, (x - high.astype(F32)).astype(BF16)


def dot3(lhs, rhs, dims):
    mul = functools.partial(lax.dot_general, dimension_numbers=dims, preferred_element_type=F32)
    return mul(lhs[0], rhs[0]) + (mul(lhs[0], rhs[1]) + mul(lhs[1], rhs[0]))


def green_kernel(
    occ, vir, eps, full, high, low, basis, basis_high, basis_low, polar, late, late_basis, total, turned, staged, arrived,
    local_sem, basis_send, basis_recv, share_send, share_recv, cross_send, cross_recv, send, recv, part_send, part_recv,
):
    row, tm = lax.axis_index("row"), lax.axis_index("tm")
    y, z = lax.div(row, 2), lax.rem(row, 2)
    step = 1 - 2 * lax.rem(tm, 2)
    before = {"row": lax.rem(y - step + 4, 4) * 2 + z, "tm": tm}
    across = {"row": y * 2 + 1 - z, "tm": tm}
    x = lax.div(tm, 8)
    beside = [{"row": row, "tm": lax.rem(tm + 8 * i, 32)} for i in range(4)]

    def block(slot, chunk=None):
        if chunk is None:
            return pl.ds(slot * ROWS, ROWS)
        return pl.ds(slot * ROWS + PARTS[chunk][0], PARTS[chunk][1])

    core = lax.rem(tm, 2)
    other_core = {"row": row, "tm": tm + 1 - 2 * core}

    def piece(slot, of, alone):
        if alone:
            return pl.ds(pl.multiple_of(slot * ROWS + of * QUARTER, QUARTER), QUARTER)
        return pl.ds(pl.multiple_of(slot * ROWS + of * QUARTER + core * (QUARTER // 2), QUARTER // 2), QUARTER // 2)

    def send_basis(src, slot, device):
        return pltpu.make_async_remote_copy(
            src, basis.at[piece(slot, x, slot == NEXT)], basis_send.at[slot], basis_recv.at[slot], device_id=device
        )

    def share_basis(slot):
        copies["basis", slot].wait_recv()
        part = basis.at[piece(slot, x, slot == NEXT)]
        for i in range(1, 4):
            copies["share", slot, i] = pltpu.make_async_remote_copy(
                part, part, share_send.at[slot, i], share_recv.at[slot, i], device_id=beside[i]
            )
            copies["share", slot, i].start()

    def cross_basis(slot):
        for i in range(1, 4):
            copies["share", slot, i].wait_recv()
        for of in range(4):
            part = basis.at[piece(slot, of, False)]
            copies["cross", slot, of] = pltpu.make_async_remote_copy(
                part, part, cross_send.at[slot, of], cross_recv.at[slot, of], device_id=other_core
            )
            copies["cross", slot, of].start()

    def take_basis(slot):
        if slot == NEXT:
            for i in range(1, 4):
                copies["share", slot, i].wait_recv()
        else:
            for of in range(4):
                copies["cross", slot, of].wait_recv()
        convert_basis(slot)

    def send_rows(which, chunk, src, slot, device):
        return pltpu.make_async_remote_copy(
            src, full.at[which, block(slot, chunk)],
            send.at[which, slot, chunk], recv.at[which, slot, chunk], device_id=device,
        )

    sources = (occ.at[0], vir.at[0])
    copies = {}
    copies["basis", NEXT] = send_basis(eps.at[piece(0, x, True)], NEXT, before)
    copies["basis", ACROSS] = send_basis(eps.at[piece(0, x, False)], ACROSS, across)
    for chunk in range(len(PARTS)):
        for which in range(2):
            part = sources[which].at[pl.ds(*PARTS[chunk])]
            copies[which, NEXT, chunk] = send_rows(which, chunk, part, NEXT, before)
            copies[which, ACROSS, chunk] = send_rows(which, chunk, part, ACROSS, across)
    for copy in copies.values():
        copy.start()

    own = [pltpu.make_async_copy(sources[which], full.at[which, block(OWN)], local_sem.at[which]) for which in range(2)]
    own.append(pltpu.make_async_copy(eps, basis.at[block(OWN)], local_sem.at[2]))
    for copy in own:
        copy.start()
    for copy in own:
        copy.wait()

    def convert(slot, first, size):
        start = slot * ROWS + first

        def body(i, carry):
            rows = pl.ds(start + i * 16, 16)
            for which in range(2):
                high[which, rows], low[which, rows] = halves_of(full[which, rows])
            return carry

        lax.fori_loop(0, size // 16, body, 0)

    def convert_basis(slot):
        def body(i, carry):
            rows = pl.ds(slot * ROWS + i * 16, 16)
            basis_high[rows], basis_low[rows] = halves_of(basis[rows])
            return carry

        lax.fori_loop(0, ROWS // 16, body, 0)

    def greens(left, size, right, width, weight):
        def one(which):
            lhs = (high[which, pl.ds(left, size)], low[which, pl.ds(left, size)])
            rhs = (high[which, pl.ds(right, width)], low[which, pl.ds(right, width)])
            return dot3(lhs, rhs, NT_DIMS)

        polar[0:size, pl.ds(right, width)] = weight * (one(0) * one(1))

    def project(left, size, spans, first):
        term = None
        for start, width in spans:
            rhs = (basis_high[pl.ds(start, width)], basis_low[pl.ds(start, width)])
            new = dot3(halves_of(polar[0:size, pl.ds(start, width)]), rhs, NN_DIMS)
            term = new if term is None else term + new
        term = halves_of(term)

        def body(i, carry):
            columns = pl.ds(pl.multiple_of(i * 256, 256), 256)
            lhs = (basis_high[pl.ds(left, size), columns], basis_low[pl.ds(left, size), columns])
            new = dot3(lhs, term, TN_DIMS)
            total[columns] = new if first else total[columns] + new
            return carry

        lax.fori_loop(0, 4, body, 0)

    def convert_late(k, slot):
        def body(i, carry):
            rows = pl.ds(slot * ROWS + EARLY + i * 16, 16)
            for which in range(2):
                upper, lower = halves_of(full[which, rows])
                late[which, pl.ds(k * LATE + i * 16, 16)] = upper
                late[which, pl.ds((2 + k) * LATE + i * 16, 16)] = lower
                if slot == ACROSS:
                    high[which, rows], low[which, rows] = upper, lower
            return carry

        lax.fori_loop(0, LATE // 16, body, 0)

    def prepare_late_basis():
        for k, slot in enumerate((ACROSS, FAR)):
            rows = basis[slot * ROWS + EARLY:(slot + 1) * ROWS]
            turned[k * LATE:(k + 1) * LATE, :] = rows
        upper, lower = halves_of(turned[0:TILE].T)
        late_basis[:, 0:TILE] = upper
        late_basis[:, TILE:2 * TILE] = upper
        late_basis[:, 2 * TILE:3 * TILE] = lower

    def late_work():
        rows = pl.ds(*MEETING)

        def one(which):
            both = lax.dot_general(high[which, rows], late[which], NT_DIMS, preferred_element_type=F32)
            rest = lax.dot_general(low[which, rows], late[which, 0:TILE], NT_DIMS, preferred_element_type=F32)
            return both[:, 0:TILE] + (both[:, TILE:] + rest)

        at_row = lax.broadcasted_iota(jnp.int32, (MEETING[1], TILE), 0)
        across_side = lax.broadcasted_iota(jnp.int32, (MEETING[1], TILE), 1) < LATE
        weight = jnp.where(
            at_row < LATE, 0.5,
            jnp.where(
                at_row < LATE + ROWS, jnp.where(across_side, 1.0, 0.0),
                jnp.where(across_side, 0.0, jnp.where(at_row < LATE + ROWS + EARLY, 1.0, 0.5)),
            ),
        )
        upper, lower = halves_of((weight * (one(0) * one(1))).T)
        both = jnp.concatenate([upper, lower], axis=0)
        term = lax.dot_general(both, basis_high[rows], NN_DIMS, preferred_element_type=F32)
        term = term[0:TILE] + (
            term[TILE:] + lax.dot_general(upper, basis_low[rows], NN_DIMS, preferred_element_type=F32)
        )
        upper, lower = halves_of(term)
        rhs = jnp.concatenate([upper, lower, upper], axis=0)

        def body(i, carry):
            part = pl.ds(pl.multiple_of(i * 256, 256), 256)
            total[part] += lax.dot_general(late_basis[part], rhs, NN_DIMS, preferred_element_type=F32)
            return carry

        lax.fori_loop(0, 4, body, 0)

    def at(slot, first=0):
        return slot * ROWS + first

    def wait_rows(slot, chunk):
        for which in range(2):
            copies[which, slot, chunk].wait_recv()

    def work(slot, first, size, spans, opening=False):
        for start, width, weight in spans:
            greens(at(slot, first), size, start, width, weight)
        project(at(slot, first), size, [span[:2] for span in spans], opening)

    convert_basis(OWN)
    share_basis(NEXT)
    copies["basis", FAR] = send_basis(basis.at[piece(NEXT, x, False)], FAR, before)
    copies["basis", FAR].start()
    share_basis(ACROSS)
    convert(OWN, 0, ROWS)
    work(OWN, 0, 128, [(at(OWN), ROWS, 0.5)], opening=True)
    work(OWN, 128, 128, [(at(OWN), ROWS, 0.5)])
    for chunk in range(len(PARTS)):
        wait_rows(NEXT, chunk)
        for which in range(2):
            copies[which, FAR, chunk] = send_rows(which, chunk, full.at[which, block(NEXT, chunk)], FAR, before)
            copies[which, FAR, chunk].start()
    share_basis(FAR)
    cross_basis(ACROSS)
    take_basis(NEXT)
    convert(NEXT, 0, ROWS)
    work(NEXT, 0, 128, [(at(OWN), ROWS, 1.0)])
    work(NEXT, 128, 128, [(at(OWN), ROWS, 1.0)])

    cross_basis(FAR)
    take_basis(ACROSS)
    take_basis(FAR)
    prepare_late_basis()
    own_weight = jnp.where(lax.broadcasted_iota(jnp.int32, (1, 2 * ROWS), 1) < EARLY, 0.5, 1.0)
    wait_rows(ACROSS, 0)
    convert(ACROSS, 0, EARLY)
    work(ACROSS, 0, EARLY, [(at(OWN), 2 * ROWS, own_weight)])
    wait_rows(FAR, 0)
    convert(FAR, 0, EARLY)
    work(FAR, 0, EARLY, [(at(OWN), ROWS, own_weight[:, 0:ROWS]), (at(ACROSS), EARLY, 0.5)])
    wait_rows(ACROSS, 1)
    convert_late(0, ACROSS)
    wait_rows(FAR, 1)
    convert_late(1, FAR)
    late_work()

    def fold(owner, slot):
        def span(j):
            return pl.ds(pl.multiple_of(j * TILE, TILE), TILE)

        rows = span(owner)
        place = ring_place(owner)
        for d in range(4):
            tile = span(ring_row(place + d))
            staged[slot, d * TILE:(d + 1) * TILE] = total[rows, tile] + total[tile, rows].T
        upper = lax.div(place, 4)
        low_tile, high_tile = ring_row(lax.rem(place, 4)), ring_row(lax.rem(place, 4) + 4)
        turned[:, 0:TILE] = total[span(high_tile), span(low_tile)].T
        half = pl.ds(pl.multiple_of(low_tile * TILE + upper * 64, 64), 64)
        staged[slot, 4 * TILE:KEPT] = (
            total[half, span(high_tile)] + turned[pl.ds(pl.multiple_of(upper * 64, 64), 64), 0:TILE]
        )

    def half_rows(half):
        return pl.ds(pl.multiple_of(half * SHARE, SHARE), SHARE)

    def part_copy(owner, i, half):
        return pltpu.make_async_remote_copy(
            staged.at[i, half_rows(half)], arrived.at[i, half_rows(half)], part_send.at[half, i], part_recv.at[half, i],
            device_id={"row": owner, "tm": tm},
        )

    def send_first(i, carry):
        owner = lax.rem(row + i, 8)
        fold(owner, i)
        part_copy(owner, i, 1 - core).start()
        return carry

    def send_second(i, carry):
        part_copy(lax.rem(row + i, 8), i, core).start()
        return carry

    lax.fori_loop(1, 8, send_first, 0)
    lax.fori_loop(1, 8, send_second, 0)
    fold(row, 0)

    def reduce_half(half, result):
        def take_part(i, carry):
            part_copy(row, i, half).wait_recv()
            return carry

        lax.fori_loop(1, 8, take_part, 0)

        def add(i, carry):
            rows = pl.ds(pl.multiple_of(half * SHARE + i * 32, 32), 32)
            value = staged[0, rows]
            for j in range(1, 8):
                value = value + arrived[j, rows]
            result[pl.ds(pl.multiple_of(i * 32, 32), 32)] = value
            return carry

        lax.fori_loop(0, SHARE // 32, add, 0)

    def finish():
        for copy in copies.values():
            copy.wait_send()

        def drain(i, carry):
            for half in range(2):
                part_copy(row, i, half).wait_send()
            return carry

        lax.fori_loop(1, 8, drain, 0)

    return reduce_half, finish


def meet():
    row, tm = lax.axis_index("row"), lax.axis_index("tm")
    chip, core = lax.div(tm, 2), lax.rem(tm, 2)
    barrier = pltpu.get_barrier_semaphore()

    def greet_row(i, carry):
        pl.semaphore_signal(barrier, inc=1, device_id={"row": lax.rem(row + i, 8), "tm": tm})
        return carry

    def greet_chip(i, carry):
        pl.semaphore_signal(barrier, inc=1, device_id={"row": row, "tm": lax.rem(chip + i, 16) * 2 + core})
        return carry

    lax.fori_loop(1, 8, greet_row, 0)
    lax.fori_loop(1, 16, greet_chip, 0)
    pl.semaphore_signal(barrier, inc=1, device_id={"row": row, "tm": chip * 2 + 1 - core})
    pl.semaphore_wait(barrier, 23)


def cosine(freq, time):
    scale = math.sqrt((1.0 if freq == 0 else 2.0) / 32)
    return scale * math.cos(math.pi * freq * (time + 0.5) / 32)


def cosine_kernel(
    reduce_half, out, for_partner, paired, times, times_more, freqs, freqs_more, gathered, gathered_more,
    final, final_more, flat, mirror, mirror_half, joined,
    swap_send, swap_recv, chip_send, chip_recv, more_send, more_recv, back_send, back_recv,
    back_more_send, back_more_recv, end_send, end_recv, mirror_send, mirror_recv,
):
    row, tm = lax.axis_index("row"), lax.axis_index("tm")
    chip, core = lax.div(tm, 2), lax.rem(tm, 2)
    partner = {"row": row, "tm": chip * 2 + 1 - core}
    has_more = lax.rem(chip, 5) == 0

    def other(i):
        return lax.rem(lax.div(chip, 4) + lax.div(i, 4), 4) * 4 + lax.rem(lax.rem(chip, 4) + lax.rem(i, 4), 4)

    def device(target):
        return {"row": row, "tm": target * 2 + core}

    def aligned(start, size):
        return pl.ds(pl.multiple_of(start, size), size)

    def wait_bytes(ref, sem):
        pltpu.make_async_copy(ref, ref, sem).wait()

    swap = pltpu.make_async_remote_copy(for_partner, paired.at[core], swap_send, swap_recv, device_id=partner)
    reduce_half(1 - core, for_partner)
    swap.start()

    def more_copy(which, e):
        return pltpu.make_async_remote_copy(
            paired.at[which, MAIN + e * 8:MAIN + e * 8 + 8], times_more.at[which, chip],
            more_send.at[which, e], more_recv.at[which], device_id=device(5 * e),
        )

    def spread(which):
        def one(i, carry):
            target = other(i)
            pltpu.make_async_remote_copy(
                paired.at[which, aligned(target * 16, 16)], times.at[which, chip],
                chip_send.at[which], chip_recv.at[which], device_id=device(target),
            ).start()
            return carry

        lax.fori_loop(1, 16, one, 0)
        for e in range(4):
            @pl.when(chip != 5 * e)
            def _():
                more_copy(which, e).start()

            @pl.when(chip == 5 * e)
            def _():
                times_more[which, chip] = paired[which, MAIN + e * 8:MAIN + e * 8 + 8]
        times[which, chip] = paired[which, aligned(chip * 16, 16)]

    swap.wait_recv()
    spread(1 - core)
    reduce_half(core, paired.at[core])
    spread(core)
    for which in range(2):
        wait_bytes(times.at[which, pl.ds(0, 15)], chip_recv.at[which])

    @pl.when(has_more)
    def _():
        for which in range(2):
            wait_bytes(times_more.at[which, pl.ds(0, 15)], more_recv.at[which])

    def transform(source, result, rows, parity):
        at = [source[t % 2, t // 2, rows] for t in range(32)]
        if parity:
            mixed = [at[t] - at[31 - t] for t in range(16)]
        else:
            mixed = [at[t] + at[31 - t] for t in range(16)]
        for freq in range(parity, 32, 2):
            value = None
            for t in range(16):
                term = cosine(freq, t) * mixed[t]
                value = term if value is None else value + term
            result[parity, freq // 2, rows] = value

    def transform_all(which):
        for parity in range(2):
            @pl.when(which == parity)
            def _():
                def main(i, carry):
                    transform(times, freqs, aligned(i * 8, 8), parity)
                    return carry

                lax.fori_loop(0, 2, main, 0)

                @pl.when(has_more)
                def _():
                    transform(times_more, freqs_more, pl.ds(0, 8), parity)

    def back_more_copy(which, target, e):
        return pltpu.make_async_remote_copy(
            freqs_more.at[which, target], gathered_more.at[which, e],
            back_more_send.at[which], back_more_recv.at[which, e], device_id=device(target),
        )

    def give(which):
        def one(i, carry):
            target = other(i)
            pltpu.make_async_remote_copy(
                freqs.at[which, target], gathered.at[which, chip],
                back_send.at[which], back_recv.at[which], device_id=device(target),
            ).start()
            return carry

        lax.fori_loop(1, 16, one, 0)

        @pl.when(has_more)
        def _():
            def one_more(i, carry):
                back_more_copy(which, other(i), lax.div(chip, 5)).start()
                return carry

            lax.fori_loop(1, 16, one_more, 0)
            gathered_more[which, lax.div(chip, 5)] = freqs_more[which, chip]

        gathered[which, chip] = freqs[which, chip]

    def take(which):
        wait_bytes(gathered.at[which, pl.ds(0, 15)], back_recv.at[which])
        for e in range(4):
            @pl.when(chip != 5 * e)
            def _():
                back_more_copy(which, chip, e).wait_recv()

    for which in (1 - core, core):
        transform_all(which)
        give(which)
    take(1 - core)
    last = pltpu.make_async_remote_copy(
        gathered.at[1 - core], final.at[core], end_send.at[0], end_recv.at[0], device_id=partner
    )
    last_more = pltpu.make_async_remote_copy(
        gathered_more.at[1 - core], final_more.at[core], end_send.at[1], end_recv.at[1], device_id=partner
    )
    last.start()
    last_more.start()
    place = ring_place(row)
    pieces = (((128, 128, 1), (256, 32, 2)), ((288, 96, 2), (384, 128, 3), (512, 64, 4)))
    mirrors = [], []
    for half in range(2):
        for start, count, d in pieces[half]:
            to = mirror_half if d == 4 else mirror.at[d - 1, pl.ds(start - d * TILE, count)]
            k = len(mirrors[0]) + len(mirrors[1])
            mirrors[half].append(pltpu.make_async_remote_copy(
                flat.at[pl.ds(start, count)], to, mirror_send.at[k], mirror_recv.at[k],
                device_id={"row": ring_row(place + d), "tm": tm},
            ))

    def complete(half):
        for p in range(16):
            flat[aligned(half * SHARE + p * 16, 16)] = final[half, p]
        for e in range(4):
            flat[aligned(half * SHARE + MAIN + e * 8, 8)] = final_more[half, e]
        for known in range(2):
            @pl.when(half == known)
            def _():
                for copy in mirrors[known]:
                    copy.start()

    last.wait_recv()
    last_more.wait_recv()
    complete(1 - core)
    take(core)
    final[core] = gathered[core]
    final_more[core] = gathered_more[core]
    complete(core)

    def columns(j):
        return aligned(ring_row(j) * TILE, TILE)

    for d in range(4):
        out[0, :, columns(place + d)] = flat[d * TILE:(d + 1) * TILE]
    for half in range(2):
        for copy in mirrors[half]:
            copy.wait_recv()
    for d in range(1, 4):
        out[0, :, columns(place + 8 - d)] = mirror[d - 1].T
    upper = lax.div(place, 4)
    joined[aligned(upper * 64, 64)] = flat[4 * TILE:KEPT]
    joined[aligned((1 - upper) * 64, 64)] = mirror_half[...]

    @pl.when(upper == 0)
    def _():
        out[0, :, columns(place + 4)] = joined[...]

    @pl.when(upper == 1)
    def _():
        out[0, :, columns(place + 4)] = joined[...].T

    for copy in [*mirrors[0], *mirrors[1], swap, last, last_more]:
        copy.wait_send()
    for which in range(2):
        wait_bytes(times.at[which, pl.ds(0, 15)], chip_send.at[which])
        wait_bytes(times.at[which, pl.ds(0, 15)], back_send.at[which])
        for e in range(4):
            @pl.when(chip != 5 * e)
            def _():
                more_copy(which, e).wait_send()

    @pl.when(has_more)
    def _():
        for which in range(2):
            wait_bytes(times_more.at[which, pl.ds(0, 15)], back_more_send.at[which])


def kernel(occ, vir, eps, out, *scratch):
    meet()
    reduce_half, finish = green_kernel(occ, vir, eps, *scratch[:GREEN_SCRATCH])
    cosine_kernel(reduce_half, out, *scratch[GREEN_SCRATCH:])
    finish()


def on_device(occ_factor, vir_factor, eps_basis):
    dma = pltpu.SemaphoreType.DMA
    main = pltpu.VMEM((2, 16, 16, TILE), F32)
    more = pltpu.VMEM((2, 16, 8, TILE), F32)
    rows_sems = dma((2, 4, len(PARTS)))
    green = [
        pltpu.VMEM((2, 4 * ROWS, 2048), F32),
        pltpu.VMEM((2, 4 * ROWS, 2048), BF16),
        pltpu.VMEM((2, 4 * ROWS, 2048), BF16),
        pltpu.VMEM((4 * ROWS, 1024), F32),
        pltpu.VMEM((4 * ROWS, 1024), BF16),
        pltpu.VMEM((4 * ROWS, 1024), BF16),
        pltpu.VMEM((EARLY, 4 * ROWS), F32),
        pltpu.VMEM((2, 4 * LATE, 2048), BF16),
        pltpu.VMEM((1024, 3 * TILE), BF16),
        pltpu.VMEM((1024, 1024), F32),
        pltpu.VMEM((TILE, 1024), F32),
        pltpu.VMEM((8, KEPT, TILE), F32),
        pltpu.VMEM((8, KEPT, TILE), F32),
        dma((3,)), dma((4,)), dma((4,)), dma((4, 4)), dma((4, 4)), dma((4, 4)), dma((4, 4)), rows_sems, rows_sems, dma((2, 8)), dma((2, 8)),
    ]
    assert len(green) == GREEN_SCRATCH
    return pl.pallas_call(
        kernel,
        out_shape=jax.ShapeDtypeStruct((1, TILE, 1024), F32),
        in_specs=[pl.BlockSpec(memory_space=pl.ANY)] * 3,
        out_specs=pl.BlockSpec(memory_space=pltpu.VMEM),
        scratch_shapes=[
            *green,
            pltpu.VMEM((SHARE, TILE), F32),
            pltpu.VMEM((2, SHARE, TILE), F32),
            main, more, main, more, main,
            pltpu.VMEM((2, 4, 8, TILE), F32),
            main,
            pltpu.VMEM((2, 4, 8, TILE), F32),
            pltpu.VMEM((KEPT, TILE), F32),
            pltpu.VMEM((3, TILE, TILE), F32),
            pltpu.VMEM((64, TILE), F32),
            pltpu.VMEM((TILE, TILE), F32),
            dma, dma, dma((2,)), dma((2,)), dma((2, 4)), dma((2,)), dma((2,)), dma((2,)), dma((2,)), dma((2, 4)), dma((2,)), dma((2,)),
            dma((5,)), dma((5,)),
        ],
        compiler_params=pltpu.CompilerParams(
            collective_id=0, has_side_effects=True, vmem_limit_bytes=59 << 20
        ),
        cost_estimate=pl.CostEstimate(flops=20 * 10**9, bytes_accessed=20 << 20, transcendentals=0),
        name="polarizability",
    )(occ_factor, vir_factor, eps_basis)


def solution(mesh):
    placed = (P("tm", "row", None), P("tm", "row", None), P("row", None))
    return jax.shard_map(
        on_device, mesh=mesh, in_specs=placed, out_specs=P("tm", "row", None), check_vma=False
    )
```

```python
import functools
import math

import jax
import jax.numpy as jnp
from jax import lax
from jax.experimental import pallas as pl
from jax.experimental.pallas import tpu as pltpu
from jax.sharding import PartitionSpec as P

F32 = jnp.float32
BF16 = jnp.bfloat16
NT_DIMS = (((1,), (1,)), ((), ()))
NN_DIMS = (((1,), (0,)), ((), ()))
TN_DIMS = (((0,), (0,)), ((), ()))
OWN, NEXT, ACROSS, FAR = 0, 1, 2, 3
ROWS = 256
EARLY, LATE = 192, 64
PARTS = ((0, EARLY), (EARLY, LATE))
MEETING = (EARLY, LATE + 2 * ROWS)
TILE = 128
QUARTER = 64
KEPT = 4 * TILE + 64
SHARE = KEPT // 2
MAIN = 256
GREEN_SCRATCH = 24


def ring_place(row):
    y, z = lax.div(row, 2), lax.rem(row, 2)
    return y + z * (7 - 2 * y)


def ring_row(place):
    place = lax.rem(place, 8)
    z = lax.div(place, 4)
    return (place + z * (7 - 2 * place)) * 2 + z


def halves_of(x):
    high = x.astype(BF16)
    return high, (x - high.astype(F32)).astype(BF16)


def dot3(lhs, rhs, dims):
    mul = functools.partial(lax.dot_general, dimension_numbers=dims, preferred_element_type=F32)
    return mul(lhs[0], rhs[0]) + (mul(lhs[0], rhs[1]) + mul(lhs[1], rhs[0]))


def green_kernel(
    occ, vir, eps, full, high, low, basis, basis_high, basis_low, polar, late, late_basis, total, turned, staged, arrived,
    local_sem, basis_send, basis_recv, share_send, share_recv, cross_send, cross_recv, send, recv, part_send, part_recv,
):
    row, tm = lax.axis_index("row"), lax.axis_index("tm")
    y, z = lax.div(row, 2), lax.rem(row, 2)
    step = 1 - 2 * lax.rem(tm, 2)
    before = {"row": lax.rem(y - step + 4, 4) * 2 + z, "tm": tm}
    across = {"row": y * 2 + 1 - z, "tm": tm}
    x = lax.div(tm, 8)
    beside = [{"row": row, "tm": lax.rem(tm + 8 * i, 32)} for i in range(4)]

    def block(slot, chunk=None):
        if chunk is None:
            return pl.ds(slot * ROWS, ROWS)
        return pl.ds(slot * ROWS + PARTS[chunk][0], PARTS[chunk][1])

    core = lax.rem(tm, 2)
    other_core = {"row": row, "tm": tm + 1 - 2 * core}

    def piece(slot, of, alone):
        if alone:
            return pl.ds(pl.multiple_of(slot * ROWS + of * QUARTER, QUARTER), QUARTER)
        return pl.ds(pl.multiple_of(slot * ROWS + of * QUARTER + core * (QUARTER // 2), QUARTER // 2), QUARTER // 2)

    def send_basis(src, slot, device):
        return pltpu.make_async_remote_copy(
            src, basis.at[piece(slot, x, slot == NEXT)], basis_send.at[slot], basis_recv.at[slot], device_id=device
        )

    def share_basis(slot):
        copies["basis", slot].wait_recv()
        part = basis.at[piece(slot, x, slot == NEXT)]
        for i in range(1, 4):
            copies["share", slot, i] = pltpu.make_async_remote_copy(
                part, part, share_send.at[slot, i], share_recv.at[slot, i], device_id=beside[i]
            )
            copies["share", slot, i].start()

    def cross_basis(slot):
        for i in range(1, 4):
            copies["share", slot, i].wait_recv()
        for of in range(4):
            part = basis.at[piece(slot, of, False)]
            copies["cross", slot, of] = pltpu.make_async_remote_copy(
                part, part, cross_send.at[slot, of], cross_recv.at[slot, of], device_id=other_core
            )
            copies["cross", slot, of].start()

    def take_basis(slot):
        if slot == NEXT:
            for i in range(1, 4):
                copies["share", slot, i].wait_recv()
        else:
            for of in range(4):
                copies["cross", slot, of].wait_recv()
        convert_basis(slot)

    def send_rows(which, chunk, src, slot, device):
        return pltpu.make_async_remote_copy(
            src, full.at[which, block(slot, chunk)],
            send.at[which, slot, chunk], recv.at[which, slot, chunk], device_id=device,
        )

    sources = (occ.at[0], vir.at[0])
    copies = {}
    copies["basis", NEXT] = send_basis(eps.at[piece(0, x, True)], NEXT, before)
    copies["basis", ACROSS] = send_basis(eps.at[piece(0, x, False)], ACROSS, across)
    for chunk in range(len(PARTS)):
        for which in range(2):
            part = sources[which].at[pl.ds(*PARTS[chunk])]
            copies[which, NEXT, chunk] = send_rows(which, chunk, part, NEXT, before)
            copies[which, ACROSS, chunk] = send_rows(which, chunk, part, ACROSS, across)
    for copy in copies.values():
        copy.start()

    own = [pltpu.make_async_copy(sources[which], full.at[which, block(OWN)], local_sem.at[which]) for which in range(2)]
    own.append(pltpu.make_async_copy(eps, basis.at[block(OWN)], local_sem.at[2]))
    for copy in own:
        copy.start()
    for copy in own:
        copy.wait()

    def convert(slot, first, size):
        start = slot * ROWS + first

        def body(i, carry):
            rows = pl.ds(start + i * 16, 16)
            for which in range(2):
                high[which, rows], low[which, rows] = halves_of(full[which, rows])
            return carry

        lax.fori_loop(0, size // 16, body, 0)

    def convert_basis(slot):
        def body(i, carry):
            rows = pl.ds(slot * ROWS + i * 16, 16)
            basis_high[rows], basis_low[rows] = halves_of(basis[rows])
            return carry

        lax.fori_loop(0, ROWS // 16, body, 0)

    def greens(left, size, right, width, weight):
        def one(which):
            lhs = (high[which, pl.ds(left, size)], low[which, pl.ds(left, size)])
            rhs = (high[which, pl.ds(right, width)], low[which, pl.ds(right, width)])
            return dot3(lhs, rhs, NT_DIMS)

        polar[0:size, pl.ds(right, width)] = weight * (one(0) * one(1))

    def project(left, size, spans, first):
        term = None
        for start, width in spans:
            rhs = (basis_high[pl.ds(start, width)], basis_low[pl.ds(start, width)])
            new = dot3(halves_of(polar[0:size, pl.ds(start, width)]), rhs, NN_DIMS)
            term = new if term is None else term + new
        term = halves_of(term)

        def body(i, carry):
            columns = pl.ds(pl.multiple_of(i * 256, 256), 256)
            lhs = (basis_high[pl.ds(left, size), columns], basis_low[pl.ds(left, size), columns])
            new = dot3(lhs, term, TN_DIMS)
            total[columns] = new if first else total[columns] + new
            return carry

        lax.fori_loop(0, 4, body, 0)

    def convert_late(k, slot):
        def body(i, carry):
            rows = pl.ds(slot * ROWS + EARLY + i * 16, 16)
            for which in range(2):
                upper, lower = halves_of(full[which, rows])
                late[which, pl.ds(k * LATE + i * 16, 16)] = upper
                late[which, pl.ds((2 + k) * LATE + i * 16, 16)] = lower
                if slot == ACROSS:
                    high[which, rows], low[which, rows] = upper, lower
            return carry

        lax.fori_loop(0, LATE // 16, body, 0)

    def prepare_late_basis():
        for k, slot in enumerate((ACROSS, FAR)):
            rows = basis[slot * ROWS + EARLY:(slot + 1) * ROWS]
            turned[k * LATE:(k + 1) * LATE, :] = rows
        upper, lower = halves_of(turned[0:TILE].T)
        late_basis[:, 0:TILE] = upper
        late_basis[:, TILE:2 * TILE] = upper
        late_basis[:, 2 * TILE:3 * TILE] = lower

    def late_work():
        rows = pl.ds(*MEETING)

        def one(which):
            both = lax.dot_general(high[which, rows], late[which], NT_DIMS, preferred_element_type=F32)
            rest = lax.dot_general(low[which, rows], late[which, 0:TILE], NT_DIMS, preferred_element_type=F32)
            return both[:, 0:TILE] + (both[:, TILE:] + rest)

        at_row = lax.broadcasted_iota(jnp.int32, (MEETING[1], TILE), 0)
        across_side = lax.broadcasted_iota(jnp.int32, (MEETING[1], TILE), 1) < LATE
        weight = jnp.where(
            at_row < LATE, 0.5,
            jnp.where(
                at_row < LATE + ROWS, jnp.where(across_side, 1.0, 0.0),
                jnp.where(across_side, 0.0, jnp.where(at_row < LATE + ROWS + EARLY, 1.0, 0.5)),
            ),
        )
        upper, lower = halves_of((weight * (one(0) * one(1))).T)
        both = jnp.concatenate([upper, lower], axis=0)
        term = lax.dot_general(both, basis_high[rows], NN_DIMS, preferred_element_type=F32)
        term = term[0:TILE] + (
            term[TILE:] + lax.dot_general(upper, basis_low[rows], NN_DIMS, preferred_element_type=F32)
        )
        upper, lower = halves_of(term)
        rhs = jnp.concatenate([upper, lower, upper], axis=0)

        def body(i, carry):
            part = pl.ds(pl.multiple_of(i * 256, 256), 256)
            total[part] += lax.dot_general(late_basis[part], rhs, NN_DIMS, preferred_element_type=F32)
            return carry

        lax.fori_loop(0, 4, body, 0)

    def at(slot, first=0):
        return slot * ROWS + first

    def wait_rows(slot, chunk):
        for which in range(2):
            copies[which, slot, chunk].wait_recv()

    def work(slot, first, size, spans, opening=False):
        for start, width, weight in spans:
            greens(at(slot, first), size, start, width, weight)
        project(at(slot, first), size, [span[:2] for span in spans], opening)

    convert_basis(OWN)
    share_basis(NEXT)
    copies["basis", FAR] = send_basis(basis.at[piece(NEXT, x, False)], FAR, before)
    copies["basis", FAR].start()
    share_basis(ACROSS)
    convert(OWN, 0, ROWS)
    work(OWN, 0, 128, [(at(OWN), ROWS, 0.5)], opening=True)
    work(OWN, 128, 128, [(at(OWN), ROWS, 0.5)])
    for chunk in range(len(PARTS)):
        wait_rows(NEXT, chunk)
        for which in range(2):
            copies[which, FAR, chunk] = send_rows(which, chunk, full.at[which, block(NEXT, chunk)], FAR, before)
            copies[which, FAR, chunk].start()
    share_basis(FAR)
    cross_basis(ACROSS)
    take_basis(NEXT)
    convert(NEXT, 0, ROWS)
    work(NEXT, 0, 128, [(at(OWN), ROWS, 1.0)])
    work(NEXT, 128, 128, [(at(OWN), ROWS, 1.0)])

    cross_basis(FAR)
    take_basis(ACROSS)
    take_basis(FAR)
    prepare_late_basis()
    own_weight = jnp.where(lax.broadcasted_iota(jnp.int32, (1, 2 * ROWS), 1) < EARLY, 0.5, 1.0)
    wait_rows(ACROSS, 0)
    convert(ACROSS, 0, EARLY)
    work(ACROSS, 0, EARLY, [(at(OWN), 2 * ROWS, own_weight)])
    wait_rows(FAR, 0)
    convert(FAR, 0, EARLY)
    work(FAR, 0, EARLY, [(at(OWN), ROWS, own_weight[:, 0:ROWS]), (at(ACROSS), EARLY, 0.5)])
    wait_rows(ACROSS, 1)
    convert_late(0, ACROSS)
    wait_rows(FAR, 1)
    convert_late(1, FAR)
    late_work()

    def fold(owner, slot, half):
        def span(j):
            return pl.ds(pl.multiple_of(j * TILE, TILE), TILE)

        rows = span(owner)
        place = ring_place(owner)

        def tile_of(d):
            tile = span(ring_row(place + d))
            return total[rows, tile] + total[tile, rows].T

        @pl.when(half == 0)
        def _():
            for d in range(2):
                staged[slot, d * TILE:(d + 1) * TILE] = tile_of(d)
            staged[slot, 2 * TILE:SHARE] = tile_of(2)[0:SHARE - 2 * TILE]

        @pl.when(half == 1)
        def _():
            staged[slot, SHARE:3 * TILE] = tile_of(2)[SHARE - 2 * TILE:]
            staged[slot, 3 * TILE:4 * TILE] = tile_of(3)
            upper = lax.div(place, 4)
            low_tile, high_tile = ring_row(lax.rem(place, 4)), ring_row(lax.rem(place, 4) + 4)
            turned[:, 0:TILE] = total[span(high_tile), span(low_tile)].T
            rows_64 = pl.ds(pl.multiple_of(low_tile * TILE + upper * 64, 64), 64)
            staged[slot, 4 * TILE:KEPT] = (
                total[rows_64, span(high_tile)] + turned[pl.ds(pl.multiple_of(upper * 64, 64), 64), 0:TILE]
            )

    def half_rows(half):
        return pl.ds(pl.multiple_of(half * SHARE, SHARE), SHARE)

    def part_copy(owner, i, half):
        return pltpu.make_async_remote_copy(
            staged.at[i, half_rows(half)], arrived.at[i, half_rows(half)], part_send.at[half, i], part_recv.at[half, i],
            device_id={"row": owner, "tm": tm},
        )

    def send_first(i, carry):
        owner = lax.rem(row + i, 8)
        fold(owner, i, 1 - core)
        part_copy(owner, i, 1 - core).start()
        return carry

    def send_second(i, carry):
        owner = lax.rem(row + i, 8)
        fold(owner, i, core)
        part_copy(owner, i, core).start()
        return carry

    lax.fori_loop(1, 8, send_first, 0)
    lax.fori_loop(1, 8, send_second, 0)
    fold(row, 0, 1 - core)
    fold(row, 0, core)

    def reduce_half(half, result):
        def take_part(i, carry):
            part_copy(row, i, half).wait_recv()
            return carry

        lax.fori_loop(1, 8, take_part, 0)

        def add(i, carry):
            rows = pl.ds(pl.multiple_of(half * SHARE + i * 32, 32), 32)
            value = staged[0, rows]
            for j in range(1, 8):
                value = value + arrived[j, rows]
            result[pl.ds(pl.multiple_of(i * 32, 32), 32)] = value
            return carry

        lax.fori_loop(0, SHARE // 32, add, 0)

    def finish():
        for copy in copies.values():
            copy.wait_send()

        def drain(i, carry):
            for half in range(2):
                part_copy(row, i, half).wait_send()
            return carry

        lax.fori_loop(1, 8, drain, 0)

    return reduce_half, finish


def meet():
    row, tm = lax.axis_index("row"), lax.axis_index("tm")
    chip, core = lax.div(tm, 2), lax.rem(tm, 2)
    barrier = pltpu.get_barrier_semaphore()

    def greet_row(i, carry):
        pl.semaphore_signal(barrier, inc=1, device_id={"row": lax.rem(row + i, 8), "tm": tm})
        return carry

    def greet_chip(i, carry):
        pl.semaphore_signal(barrier, inc=1, device_id={"row": row, "tm": lax.rem(chip + i, 16) * 2 + core})
        return carry

    lax.fori_loop(1, 8, greet_row, 0)
    lax.fori_loop(1, 16, greet_chip, 0)
    pl.semaphore_signal(barrier, inc=1, device_id={"row": row, "tm": chip * 2 + 1 - core})
    pl.semaphore_wait(barrier, 23)


def cosine(freq, time):
    scale = math.sqrt((1.0 if freq == 0 else 2.0) / 32)
    return scale * math.cos(math.pi * freq * (time + 0.5) / 32)


def cosine_kernel(
    reduce_half, out, for_partner, paired, times, times_more, freqs, freqs_more, gathered, gathered_more,
    final, final_more, flat, mirror, mirror_half, joined,
    swap_send, swap_recv, chip_send, chip_recv, more_send, more_recv, back_send, back_recv,
    back_more_send, back_more_recv, end_send, end_recv, mirror_send, mirror_recv,
):
    row, tm = lax.axis_index("row"), lax.axis_index("tm")
    chip, core = lax.div(tm, 2), lax.rem(tm, 2)
    partner = {"row": row, "tm": chip * 2 + 1 - core}
    has_more = lax.rem(chip, 5) == 0

    def other(i):
        return lax.rem(lax.div(chip, 4) + lax.div(i, 4), 4) * 4 + lax.rem(lax.rem(chip, 4) + lax.rem(i, 4), 4)

    def device(target):
        return {"row": row, "tm": target * 2 + core}

    def aligned(start, size):
        return pl.ds(pl.multiple_of(start, size), size)

    def wait_bytes(ref, sem):
        pltpu.make_async_copy(ref, ref, sem).wait()

    swap = pltpu.make_async_remote_copy(for_partner, paired.at[core], swap_send, swap_recv, device_id=partner)
    reduce_half(1 - core, for_partner)
    swap.start()

    def more_copy(which, e):
        return pltpu.make_async_remote_copy(
            paired.at[which, MAIN + e * 8:MAIN + e * 8 + 8], times_more.at[which, chip],
            more_send.at[which, e], more_recv.at[which], device_id=device(5 * e),
        )

    def spread(which):
        def one(i, carry):
            target = other(i)
            pltpu.make_async_remote_copy(
                paired.at[which, aligned(target * 16, 16)], times.at[which, chip],
                chip_send.at[which], chip_recv.at[which], device_id=device(target),
            ).start()
            return carry

        lax.fori_loop(1, 16, one, 0)
        for e in range(4):
            @pl.when(chip != 5 * e)
            def _():
                more_copy(which, e).start()

            @pl.when(chip == 5 * e)
            def _():
                times_more[which, chip] = paired[which, MAIN + e * 8:MAIN + e * 8 + 8]
        times[which, chip] = paired[which, aligned(chip * 16, 16)]

    swap.wait_recv()
    spread(1 - core)
    reduce_half(core, paired.at[core])
    spread(core)
    for which in range(2):
        wait_bytes(times.at[which, pl.ds(0, 15)], chip_recv.at[which])

    @pl.when(has_more)
    def _():
        for which in range(2):
            wait_bytes(times_more.at[which, pl.ds(0, 15)], more_recv.at[which])

    def transform(source, result, rows, parity):
        at = [source[t % 2, t // 2, rows] for t in range(32)]
        if parity:
            mixed = [at[t] - at[31 - t] for t in range(16)]
        else:
            mixed = [at[t] + at[31 - t] for t in range(16)]
        for freq in range(parity, 32, 2):
            value = None
            for t in range(16):
                term = cosine(freq, t) * mixed[t]
                value = term if value is None else value + term
            result[parity, freq // 2, rows] = value

    def transform_all(which):
        for parity in range(2):
            @pl.when(which == parity)
            def _():
                def main(i, carry):
                    transform(times, freqs, aligned(i * 8, 8), parity)
                    return carry

                lax.fori_loop(0, 2, main, 0)

                @pl.when(has_more)
                def _():
                    transform(times_more, freqs_more, pl.ds(0, 8), parity)

    def back_more_copy(which, target, e):
        return pltpu.make_async_remote_copy(
            freqs_more.at[which, target], gathered_more.at[which, e],
            back_more_send.at[which], back_more_recv.at[which, e], device_id=device(target),
        )

    def give(which):
        def one(i, carry):
            target = other(i)
            pltpu.make_async_remote_copy(
                freqs.at[which, target], gathered.at[which, chip],
                back_send.at[which], back_recv.at[which], device_id=device(target),
            ).start()
            return carry

        lax.fori_loop(1, 16, one, 0)

        @pl.when(has_more)
        def _():
            def one_more(i, carry):
                back_more_copy(which, other(i), lax.div(chip, 5)).start()
                return carry

            lax.fori_loop(1, 16, one_more, 0)
            gathered_more[which, lax.div(chip, 5)] = freqs_more[which, chip]

        gathered[which, chip] = freqs[which, chip]

    def take(which):
        wait_bytes(gathered.at[which, pl.ds(0, 15)], back_recv.at[which])
        for e in range(4):
            @pl.when(chip != 5 * e)
            def _():
                back_more_copy(which, chip, e).wait_recv()

    for which in (1 - core, core):
        transform_all(which)
        give(which)
    take(1 - core)
    last = pltpu.make_async_remote_copy(
        gathered.at[1 - core], final.at[core], end_send.at[0], end_recv.at[0], device_id=partner
    )
    last_more = pltpu.make_async_remote_copy(
        gathered_more.at[1 - core], final_more.at[core], end_send.at[1], end_recv.at[1], device_id=partner
    )
    last.start()
    last_more.start()
    place = ring_place(row)
    pieces = (((128, 128, 1), (256, 32, 2)), ((288, 96, 2), (384, 128, 3), (512, 64, 4)))
    mirrors = [], []
    for half in range(2):
        for start, count, d in pieces[half]:
            to = mirror_half if d == 4 else mirror.at[d - 1, pl.ds(start - d * TILE, count)]
            k = len(mirrors[0]) + len(mirrors[1])
            mirrors[half].append(pltpu.make_async_remote_copy(
                flat.at[pl.ds(start, count)], to, mirror_send.at[k], mirror_recv.at[k],
                device_id={"row": ring_row(place + d), "tm": tm},
            ))

    def complete(half):
        for p in range(16):
            flat[aligned(half * SHARE + p * 16, 16)] = final[half, p]
        for e in range(4):
            flat[aligned(half * SHARE + MAIN + e * 8, 8)] = final_more[half, e]
        for known in range(2):
            @pl.when(half == known)
            def _():
                for copy in mirrors[known]:
                    copy.start()

    last.wait_recv()
    last_more.wait_recv()
    complete(1 - core)
    take(core)
    final[core] = gathered[core]
    final_more[core] = gathered_more[core]
    complete(core)

    def columns(j):
        return aligned(ring_row(j) * TILE, TILE)

    for d in range(4):
        out[0, :, columns(place + d)] = flat[d * TILE:(d + 1) * TILE]
    for half in range(2):
        for copy in mirrors[half]:
            copy.wait_recv()
    for d in range(1, 4):
        out[0, :, columns(place + 8 - d)] = mirror[d - 1].T
    upper = lax.div(place, 4)
    joined[aligned(upper * 64, 64)] = flat[4 * TILE:KEPT]
    joined[aligned((1 - upper) * 64, 64)] = mirror_half[...]

    @pl.when(upper == 0)
    def _():
        out[0, :, columns(place + 4)] = joined[...]

    @pl.when(upper == 1)
    def _():
        out[0, :, columns(place + 4)] = joined[...].T

    for copy in [*mirrors[0], *mirrors[1], swap, last, last_more]:
        copy.wait_send()
    for which in range(2):
        wait_bytes(times.at[which, pl.ds(0, 15)], chip_send.at[which])
        wait_bytes(times.at[which, pl.ds(0, 15)], back_send.at[which])
        for e in range(4):
            @pl.when(chip != 5 * e)
            def _():
                more_copy(which, e).wait_send()

    @pl.when(has_more)
    def _():
        for which in range(2):
            wait_bytes(times_more.at[which, pl.ds(0, 15)], back_more_send.at[which])


def kernel(occ, vir, eps, out, *scratch):
    meet()
    reduce_half, finish = green_kernel(occ, vir, eps, *scratch[:GREEN_SCRATCH])
    cosine_kernel(reduce_half, out, *scratch[GREEN_SCRATCH:])
    finish()


def on_device(occ_factor, vir_factor, eps_basis):
    dma = pltpu.SemaphoreType.DMA
    main = pltpu.VMEM((2, 16, 16, TILE), F32)
    more = pltpu.VMEM((2, 16, 8, TILE), F32)
    rows_sems = dma((2, 4, len(PARTS)))
    green = [
        pltpu.VMEM((2, 4 * ROWS, 2048), F32),
        pltpu.VMEM((2, 4 * ROWS, 2048), BF16),
        pltpu.VMEM((2, 4 * ROWS, 2048), BF16),
        pltpu.VMEM((4 * ROWS, 1024), F32),
        pltpu.VMEM((4 * ROWS, 1024), BF16),
        pltpu.VMEM((4 * ROWS, 1024), BF16),
        pltpu.VMEM((EARLY, 4 * ROWS), F32),
        pltpu.VMEM((2, 4 * LATE, 2048), BF16),
        pltpu.VMEM((1024, 3 * TILE), BF16),
        pltpu.VMEM((1024, 1024), F32),
        pltpu.VMEM((TILE, 1024), F32),
        pltpu.VMEM((8, KEPT, TILE), F32),
        pltpu.VMEM((8, KEPT, TILE), F32),
        dma((3,)), dma((4,)), dma((4,)), dma((4, 4)), dma((4, 4)), dma((4, 4)), dma((4, 4)), rows_sems, rows_sems, dma((2, 8)), dma((2, 8)),
    ]
    assert len(green) == GREEN_SCRATCH
    return pl.pallas_call(
        kernel,
        out_shape=jax.ShapeDtypeStruct((1, TILE, 1024), F32),
        in_specs=[pl.BlockSpec(memory_space=pl.ANY)] * 3,
        out_specs=pl.BlockSpec(memory_space=pltpu.VMEM),
        scratch_shapes=[
            *green,
            pltpu.VMEM((SHARE, TILE), F32),
            pltpu.VMEM((2, SHARE, TILE), F32),
            main, more, main, more, main,
            pltpu.VMEM((2, 4, 8, TILE), F32),
            main,
            pltpu.VMEM((2, 4, 8, TILE), F32),
            pltpu.VMEM((KEPT, TILE), F32),
            pltpu.VMEM((3, TILE, TILE), F32),
            pltpu.VMEM((64, TILE), F32),
            pltpu.VMEM((TILE, TILE), F32),
            dma, dma, dma((2,)), dma((2,)), dma((2, 4)), dma((2,)), dma((2,)), dma((2,)), dma((2,)), dma((2, 4)), dma((2,)), dma((2,)),
            dma((5,)), dma((5,)),
        ],
        compiler_params=pltpu.CompilerParams(
            collective_id=0, has_side_effects=True, vmem_limit_bytes=59 << 20
        ),
        cost_estimate=pl.CostEstimate(flops=20 * 10**9, bytes_accessed=20 << 20, transcendentals=0),
        name="polarizability",
    )(occ_factor, vir_factor, eps_basis)


def solution(mesh):
    placed = (P("tm", "row", None), P("tm", "row", None), P("row", None))
    return jax.shard_map(
        on_device, mesh=mesh, in_specs=placed, out_specs=P("tm", "row", None), check_vma=False
    )
```
